256 devices in a mesh: chan: 16 (over y_lo, z), seg: 16 (over y_hi, x, core).
Axes of the slice: x: 4, y: 4 (y_hi: 2, y_lo: 2; y = y_hi * 2 + y_lo), z: 8, core: 2. Of those that a mesh axis runs over, the one named last changes fastest.
Arguments:
- traces: bfloat16 [2048, 32768], P('chan', 'seg'), may hold values from -36 to 36
- pair_bins: int32 [2, 2048, 128], P(None, 'chan'), may hold values from 0 to 255
Outputs:
- correlograms: float32 [65, 256], P(None, 'chan')
The draws below stay inside these ranges and needn't reach their ends.
All inputs are finite; a program needn't handle non-finite values.
Results may differ from the reference program's by a relative error of at most 0.0029.
Values may be sent and summed in bfloat16 or wider, within the bound.
No kernel may reach another device: no remote copies, remote signals or barrier semaphores. Data moves between devices by JAX's collectives and lax.ppermute only.
A program may use at most 64 MiB of HBM per device.

```python
import math
import jax
import jax.numpy as jnp
from jax import lax

CB = 128
SEG_LEN = 2048
MAX_LAG = 32
NB = 256
ROUNDS = 2
LAGS = 65
CHANNELS = 2048
TIME = 32768
PAIRS_BIN = 2048
N_CHAN = 16
N_SEG = 16


def draw_traces(key, part):
    key_gain = jax.random.fold_in(key, 11)
    key_noise = jax.random.fold_in(key, 12)
    position = jnp.arange(TIME, dtype=jnp.float32) / (TIME - 1)
    gains = jnp.exp(jax.random.uniform(key_gain, (CHANNELS, 1), jnp.float32, math.log(0.3), math.log(3.0)))
    noise = jax.random.truncated_normal(key_noise, -4.0, 4.0, (CHANNELS, TIME), jnp.float32)
    envelope = 1.0 + 2.0 * position
    return (gains * envelope[None, :] * noise).astype(jnp.bfloat16)


def place_ends(drawn, rng, least, top_value):
    index_at = [jax.random.randint(jax.random.fold_in(rng, axis), (), 0, length) for axis, length in enumerate(drawn.shape)]
    widest = drawn.shape.index(max(drawn.shape))
    neighbour = index_at[:widest] + [(index_at[widest] + 1) % drawn.shape[widest]] + index_at[widest + 1:]
    return drawn.at[tuple(index_at)].set(least).at[tuple(neighbour)].set(top_value)


def setup_inputs(seed: int = 0) -> dict:
    key_list = jax.random.split(jax.random.key(seed), 3)
    traces = draw_traces(jax.random.fold_in(key_list[2], 71), 0)
    pair_bins = place_ends(jax.random.randint(key_list[1], (ROUNDS, CHANNELS, CB), 0, NB), jax.random.fold_in(key_list[1], 1), 0, NB - 1).astype(jnp.int32)
    return dict(traces=traces, pair_bins=pair_bins)


EPSILON = 1e-06

def segment_bins(own_block, partner, own_scale, partner_scale, round_bins):
    padded = jnp.pad(partner.astype(jnp.float32), ((0, 0), (MAX_LAG, MAX_LAG)))
    offsets = jnp.arange(LAGS, dtype=jnp.int32)
    shifted = jax.vmap(lambda offset: lax.dynamic_slice_in_dim(padded, offset, SEG_LEN, 1))(offsets)
    raw_sums = jnp.einsum('at,lbt->alb', own_block.astype(jnp.float32), shifted)
    zscore = raw_sums * own_scale[:, None, None] * partner_scale[None, None, :] * (1.0 / math.sqrt(TIME))
    rounded = lax.optimization_barrier(zscore.astype(jnp.bfloat16)).astype(jnp.float32)
    bin_ids = jnp.arange(NB, dtype=jnp.int32)
    onehot = (round_bins[:, :, None] == bin_ids[None, None, :]).astype(jnp.float32)
    return jnp.einsum('alb,abn->ln', rounded, onehot)

def reference(traces, pair_bins):
    squares = lax.optimization_barrier(jnp.sum(jnp.square(traces.astype(jnp.float32)), axis=1))
    inv_rms = lax.rsqrt(squares / TIME + EPSILON)
    blocks = traces.reshape(N_CHAN, CB, N_SEG, SEG_LEN)
    scales = inv_rms.reshape(N_CHAN, CB)
    bin_blocks = pair_bins.reshape(ROUNDS, N_CHAN, CB, CB)
    total = jnp.zeros((LAGS, NB), jnp.float32)
    for round_index in range(ROUNDS):
        distance = N_CHAN // 2 - round_index

        def step_pair(carry, flat_index):
            block_index = flat_index // N_SEG
            segment = flat_index % N_SEG
            partner_index = (block_index + distance) % N_CHAN
            own_block = blocks[block_index, :, segment, :]
            partner = blocks[partner_index, :, segment, :]
            term = segment_bins(own_block, partner, scales[block_index], scales[partner_index], bin_blocks[round_index, block_index])
            return (carry + term, None)
        total, _ = lax.scan(step_pair, total, jnp.arange(N_CHAN * N_SEG, dtype=jnp.int32))
    return total * (1.0 / math.sqrt(PAIRS_BIN))
```

```python
import functools, math
import jax, jax.numpy as jnp
from jax import lax
from jax.sharding import PartitionSpec as P
from jax.experimental import pallas as pl
from jax.experimental.pallas import tpu as pltpu
NT = (((1,), (1,)), ((), ()))
F32, BF = jnp.float32, jnp.bfloat16
W = 1152

def corr_kernel(slot_ref, a0, a1, a2, b_ref, c_ref, c0_ref, a32, lbuf, bbuf):
    k = pl.program_id(0)
    @pl.when(k == 0)
    def _():
        for s in range(2):
            bp = b_ref[s].astype(F32)
            for p in range(8):
                r = bp if p == 0 else pltpu.roll(bp, 8 * p, 1)
                bbuf[s, 128 * p:128 * p + 128, :] = r.astype(BF)
    for kk, a in enumerate((a0, a1, a2)):
        @pl.when(k == kk)
        def _():
            a32[...] = a[...].astype(F32)
    slot = slot_ref[k]
    def blk(ib, _):
        rows = []
        for ii in range(16):
            x = a32[pl.ds(ib * 16 + ii, 1), :]
            x = jnp.broadcast_to(x, (8, W))
            rows.append(pltpu.roll(x, 24, 1, stride=1, stride_axis=0))
        lbuf[pl.ds(pl.multiple_of(ib * 128, 128), 128), :] = jnp.concatenate(rows, 0).astype(BF)
        return 0
    lax.fori_loop(0, 8, blk, 0)
    a_s = pltpu.roll(a32[...], 32, 1).astype(BF)
    c0_ref[0] = lax.dot_general(a_s, b_ref[slot], NT, preferred_element_type=F32)
    for mc in range(4):
        c_ref[0, 256 * mc:256 * mc + 256, :] = lax.dot_general(
            lbuf[256 * mc:256 * mc + 256, :], bbuf[slot], NT, preferred_element_type=F32)

def corr(slots, a0, a1, a2, b):
    vm = lambda shape: pl.BlockSpec(shape, lambda k, *_: (0,) * len(shape))
    return pl.pallas_call(
        corr_kernel,
        grid_spec=pltpu.PrefetchScalarGridSpec(
            num_scalar_prefetch=1, grid=(3,),
            in_specs=[vm((128, W))] * 3 + [vm((2, 128, W))],
            out_specs=[pl.BlockSpec((1, 1024, 1024), lambda k, *_: (k, 0, 0)),
                       pl.BlockSpec((1, 128, 128), lambda k, *_: (k, 0, 0))],
            scratch_shapes=[pltpu.VMEM((128, W), F32), pltpu.VMEM((1024, W), BF), pltpu.VMEM((2, 1024, W), BF)]),
        out_shape=[jax.ShapeDtypeStruct((3, 1024, 1024), F32), jax.ShapeDtypeStruct((3, 128, 128), F32)],
        compiler_params=pltpu.CompilerParams(vmem_limit_bytes=20 << 20),
        cost_estimate=pl.CostEstimate(flops=3 * 2 * 1024 * 1024 * W, bytes_accessed=13 << 20, transcendentals=0),
        name="lag_products",
    )(slots, a0, a1, a2, b)


def bin_kernel(c_ref, c0_ref, scl_ref, bins_ref, out_ref, s_buf, hi, lo, acc):
    k = pl.program_id(0); g = pl.program_id(1)
    @pl.when((k == 0) & (g == 0))
    def _():
        for t in range(3):
            col = jnp.transpose(jnp.broadcast_to(scl_ref[t:t + 1, :], (128, 128)))
            s_buf[t] = col * scl_ref[3 + t:4 + t, :]
        for t in range(4):
            b = bins_ref[t].astype(F32)
            if t % 2 == 0:
                b = jnp.transpose(b)
            h = jnp.floor(b * 0.5)
            hi[t] = h
            lo[t] = b - 2.0 * h
        acc[...] = jnp.zeros_like(acc)
    iota = lax.broadcasted_iota(jnp.int32, (128, 128), 0).astype(F32).astype(BF)
    sub16 = lax.broadcasted_iota(jnp.int32, (16, 128), 0)
    def process(t, a):
        for half in range(2):
            ohs, ws = [], []
            for ii in range(8 * half, 8 * half + 8):
                i = g * 16 + ii
                ct = c_ref[0, 8 * ii:8 * ii + 8, :]
                srow = s_buf[k, pl.ds(i, 1), :]
                z = jnp.concatenate([ct[:, 128 * p:128 * p + 128] for p in range(8)], 0) * srow
                z = z.astype(BF)
                lrow = jnp.broadcast_to(lo[t, pl.ds(i, 1), :], (64, 128)).astype(BF)
                zero = jnp.zeros((64, 128), BF)
                m = lrow == jnp.ones((64, 128), BF)
                z1 = jnp.where(m, z, zero)
                z0 = jnp.where(m, zero, z)
                x0 = c0_ref[0, pl.ds(i, 1), :] * srow
                l1 = lo[t, pl.ds(i, 1), :]
                ex = jnp.where(sub16 == 0, x0 * (1.0 - l1), jnp.where(sub16 == 1, x0 * l1, 0.0)).astype(BF)
                ws.append(jnp.concatenate([z0, z1, ex], 0))
                hrow = jnp.broadcast_to(hi[t, pl.ds(i, 1), :], (128, 128)).astype(BF)
                ohs.append(jnp.where(hrow == iota, jnp.ones((128, 128), BF), jnp.zeros((128, 128), BF)))
            acc[a] += lax.dot_general(jnp.concatenate(ohs, 1), jnp.concatenate(ws, 1), NT, preferred_element_type=F32)
    @pl.when(k == 0)
    def _():
        process(0, 0)
        process(1, 1)
    @pl.when(k == 1)
    def _():
        process(2, 0)
    @pl.when(k == 2)
    def _():
        process(3, 1)
    @pl.when((k == 2) & (g == 7))
    def _():
        c = lax.broadcasted_iota(jnp.int32, (144, 256), 0)
        o = lax.broadcasted_iota(jnp.int32, (144, 256), 1)
        r = c & 63
        m = jnp.where(c < 128, (r >> 3) * 8 + 8 - (r & 7), 0)
        lob = jnp.where(c < 128, c >> 6, c & 1)
        ok = c < 130
        out = jnp.zeros((128, 256), F32)
        for a in range(2):
            l = m if a == 0 else 64 - m
            perm = jnp.where(ok & (o == lob * 128 + l), 1.0, 0.0)
            out = out + lax.dot_general(acc[a], perm, (((1,), (0,)), ((), ())), precision=lax.Precision.HIGHEST, preferred_element_type=F32)
        out_ref[...] = out

def binning(c, c0, scl, bins):
    full = lambda shape: pl.BlockSpec(shape, lambda k, g: (0,) * len(shape))
    return pl.pallas_call(
        bin_kernel, grid=(3, 8),
        in_specs=[pl.BlockSpec((1, 128, 1024), lambda k, g: (k, g, 0)),
                  pl.BlockSpec((1, 128, 128), lambda k, g: (k, 0, 0)),
                  full((8, 128)), full((4, 128, 128))],
        out_specs=full((128, 256)),
        out_shape=jax.ShapeDtypeStruct((128, 256), F32),
        scratch_shapes=[pltpu.VMEM((3, 128, 128), F32), pltpu.VMEM((4, 128, 128), F32), pltpu.VMEM((4, 128, 128), F32),
                        pltpu.VMEM((2, 128, 144), F32)],
        compiler_params=pltpu.CompilerParams(vmem_limit_bytes=20 << 20),
        cost_estimate=pl.CostEstimate(flops=4 * 2 * 128 * 144 * 16384, bytes_accessed=13 << 20, transcendentals=0),
        name="binning",
    )(c, c0, scl, bins)


MAX_LAG = 32
NB = 256
ROUNDS = 2
EPSILON = 1e-06


def exchange(block, source):
    n = lax.axis_size("chan")
    return lax.ppermute(block, "chan", [(source(i), i) for i in range(n)])


def share(block, axis):
    n = lax.axis_size(axis)
    copies = jnp.broadcast_to(block[None], (n,) + block.shape)
    return lax.all_to_all(copies, axis, 0, 0, tiled=True)


def local(traces, pair_bins):
    channels, seg_length = traces.shape
    half_length = seg_length // 2
    total_time = seg_length * lax.axis_size("seg")
    chan_count = lax.axis_size("chan")
    index = lax.axis_index("chan")
    half = index // 8
    first = (index % 8) == 0
    last = (index % 8) == 7
    halves = (traces[:, :half_length], traces[:, half_length:])
    lane = lax.broadcasted_iota(jnp.int32, (channels, 128), 1)
    none = jnp.zeros((channels, 128), traces.dtype)
    halo_low = jnp.where(lane < MAX_LAG, traces[:, half_length:half_length + 128], none)
    halo_high = jnp.where(lane >= 128 - MAX_LAG, traces[:, half_length - 128:half_length], none)
    upper = half == 1
    mine = jnp.where(upper, halves[1], halves[0])
    other = jnp.where(upper, halves[0], halves[1])
    stream_mine, stream_other = jnp.where(upper, none, halo_low), jnp.where(upper, halo_low, none)
    held_mine, held_other = jnp.where(upper, halo_high, none), jnp.where(upper, none, halo_high)
    stream = jnp.concatenate([mine, stream_mine], 1)
    bins = pair_bins.astype(jnp.bfloat16)
    with jax.named_scope("send_blocks"):
        far = exchange(jnp.concatenate([other, held_other, bins[0], bins[1]], 1), lambda i: i ^ 8)
        lower_block = exchange(stream, lambda i: (i & 8) | ((i - 1) & 7))
        upper_payload = jnp.concatenate(
            [jnp.where(first, other, mine), jnp.where(first, stream_other, stream_mine), bins[1]], 1)
        upper_block = exchange(upper_payload, lambda i: (i & 8) | ((i + 1) & 7))
    squares = jnp.sum(jnp.square(traces.astype(jnp.float32)), axis=1)
    with jax.named_scope("energies"):
        energy = jnp.sum(share(squares[None, :], "seg"), axis=0)
        own_scale = lax.rsqrt(energy / total_time + EPSILON)
    with jax.named_scope("send_scales"):
        far_scale = exchange(own_scale, lambda i: i ^ 8)
        lower_scale = exchange(own_scale, lambda i: (i & 8) | ((i - 1) & 7))
        upper_scale = exchange(own_scale, lambda i: (i & 8) | ((i + 1) & 7))
    far_block = far[:, :W]
    far_bins0, far_bins1 = far[:, W:W + 128], far[:, W + 128:]
    special = jnp.concatenate([jnp.where(last, other, mine), jnp.where(last, held_other, held_mine)], 1)
    slots = jnp.stack([jnp.int32(0), first.astype(jnp.int32), last.astype(jnp.int32)])
    products, first_lag = corr(slots, stream, lower_block, upper_block[:, :W], jnp.stack([far_block, special]))
    time_scale = 1.0 / math.sqrt(total_time)
    scales = jnp.concatenate([
        own_scale, lower_scale, upper_scale,
        far_scale * time_scale,
        jnp.where(first, own_scale, far_scale) * time_scale,
        jnp.where(last, own_scale, far_scale) * time_scale,
        jnp.zeros((2, channels), jnp.float32)], 0)
    bin_sets = jnp.stack([far_bins0, bins[0], jnp.where(first, bins[1], far_bins1), upper_block[:, W:]])
    partial_stack = binning(products, first_lag, scales, bin_sets)
    with jax.named_scope("reduce_bins"):
        slots_out = partial_stack.reshape(chan_count, NB // chan_count // 2, 256)
        owned = jnp.sum(lax.all_to_all(slots_out, "chan", 0, 0, tiled=True), axis=0)
        owned = jnp.sum(share(owned, "seg"), axis=0)
    pair_total = ROUNDS * chan_count * channels * channels // NB
    owned = owned.reshape(-1, 2, 128)[:, :, :2 * MAX_LAG + 1] * (1.0 / math.sqrt(pair_total))
    return jnp.transpose(owned, (2, 0, 1)).reshape(2 * MAX_LAG + 1, -1)


def solution(mesh):
    in_specs = (P("chan", "seg"), P(None, "chan", None))
    out_specs = P(None, "chan")
    return jax.shard_map(local, mesh=mesh, in_specs=in_specs, out_specs=out_specs, check_vma=False)
```

```python
import functools
import math

import jax
import jax.numpy as jnp
from jax import lax
from jax.experimental import pallas as pl
from jax.experimental.pallas import tpu as pltpu
from jax.sharding import PartitionSpec as P

NT = (((1,), (1,)), ((), ()))
NN = (((1,), (0,)), ((), ()))
F32, BF = jnp.float32, jnp.bfloat16
W = 1152
CB = 128
VMEM = pl.BlockSpec(memory_space=pltpu.VMEM)
SMEM = pl.BlockSpec(memory_space=pltpu.SMEM)


def lag_rows(ref, start, count):
    rows = []
    for ii in range(count):
        x = jnp.broadcast_to(ref[pl.ds(start + ii, 1), :], (8, W))
        rows.append(pltpu.roll(x, 24, 1, stride=1, stride_axis=0))
    return jnp.concatenate(rows, 0).astype(BF)


def shift_rows(block, out_ref):
    for p in range(8):
        out_ref[CB * p:CB * p + CB, :] = block if p == 0 else pltpu.roll(block, 8 * p, 1)


GROUP = 8
CHUNK = 256


def fused_kernel(time_scale, flags, scale_ref, bins_ref, stream, lower, upper, far, special, out_ref,
                 wide, lags, shifted, c_ref, c0_ref, pair_scale, hi, lo, acc0, acc1):
    shift_rows(far[:, :W], shifted.at[0])
    shift_rows(special[...], shifted.at[1])
    wide[0] = stream[...].astype(F32)
    wide[1] = lower[...].astype(F32)
    wide[2] = upper[:, :W].astype(F32)
    first, last = flags[1] == 1, flags[2] == 1
    own, far_scale = scale_ref[0:1, :], scale_ref[1:2, :]
    held = (far_scale, jnp.where(first, own, far_scale), jnp.where(last, own, far_scale))
    for t, streamed in enumerate((own, scale_ref[2:3, :], scale_ref[3:4, :])):
        column = jnp.transpose(jnp.broadcast_to(streamed, (CB, CB)))
        pair_scale[t] = column * (held[t] * time_scale)
    sets = (far[:, W:W + CB].astype(F32), bins_ref[0].astype(F32),
            jnp.where(first, bins_ref[1].astype(F32), far[:, W + CB:].astype(F32)), upper[:, W:].astype(F32))
    for t, b in enumerate(sets):
        if t % 2 == 0:
            b = jnp.transpose(b)
        h = jnp.floor(b * 0.5)
        hi[t] = h
        lo[t] = b - 2.0 * h
    acc0[...] = jnp.zeros_like(acc0)
    acc1[...] = jnp.zeros_like(acc1)
    iota = lax.broadcasted_iota(jnp.int32, (CB, CB), 0).astype(F32).astype(BF)
    one, zero = jnp.ones((CB, CB), BF), jnp.zeros((CB, CB), BF)
    sub = lax.broadcasted_iota(jnp.int32, (32, CB), 0) & 7
    slots = (0, flags[1], flags[2])
    for k, block in enumerate((stream[...], lower[...], upper[:, :W])):
        c0_ref[k] = lax.dot_general(pltpu.roll(block, 32, 1), shifted[slots[k], :CB, :], NT, preferred_element_type=F32)

    def zscore(k, i):
        rows = c_ref[k, 8 * i:8 * i + 8, :]
        z = jnp.concatenate([rows[:, CB * p:CB * p + CB] for p in range(8)], 0)
        return (z * pair_scale[k, i:i + 1, :]).astype(BF)

    def low(t, i):
        return jnp.broadcast_to(lo[t, i:i + 1, :], (64, CB)).astype(BF)

    def onehot(t, i):
        return jnp.where(jnp.broadcast_to(hi[t, i:i + 1, :], (CB, CB)).astype(BF) == iota, one, zero)

    def bin_group(base):
        rows = pl.ds(base, GROUP)
        x = [c0_ref[k, rows, :] * pair_scale[k, rows, :] for k in range(3)]
        low8 = [lo[t, rows, :] for t in range(4)]
        extra0 = jnp.concatenate([x[0], x[0] * low8[0], x[0] * low8[1], jnp.zeros_like(x[0])], 0)
        extra1 = jnp.concatenate([x[1], x[1] * low8[2], x[2], x[2] * low8[3]], 0)
        left0, left1, right0, right1 = [], [], [], []
        for ii in range(GROUP):
            i = base + ii
            e0 = jnp.where(sub == ii, extra0, 0.0).astype(BF)
            e1 = jnp.where(sub == ii, extra1, 0.0).astype(BF)
            z = [zscore(k, i) for k in range(3)]
            left0.append(jnp.concatenate([z[0], z[0] * low(0, i), z[0] * low(1, i), e0], 0))
            left1.append(jnp.concatenate([z[1], z[1] * low(2, i), z[2], z[2] * low(3, i), e1], 0))
            right0.append(jnp.concatenate([onehot(0, i), onehot(1, i)], 0))
            right1.append(jnp.concatenate([onehot(2, i), onehot(3, i)], 0))
        cat = lambda blocks: jnp.concatenate(blocks, 1)
        acc0[...] += lax.dot_general(cat(left0), cat(right0), NT, preferred_element_type=F32)
        acc1[...] += lax.dot_general(cat(left1), cat(right1), NT, preferred_element_type=F32)

    def bin_chunk(m):
        for g in range(CHUNK // 8 // GROUP):
            bin_group(m * (CHUNK // 8) + g * GROUP)

    for m in range(1024 // CHUNK):
        rows = slice(m * CHUNK, (m + 1) * CHUNK)
        for k in range(3):
            lags[k, rows, :] = lag_rows(wide.at[k], m * CHUNK // 8, CHUNK // 8)
            c_ref[k, rows, :] = lax.dot_general(lags[k, rows, :], shifted[slots[k]], NT, preferred_element_type=F32)
        if m > 0:
            bin_chunk(m - 1)
    bin_chunk(1024 // CHUNK - 1)

    total = lambda v: jnp.sum(v, axis=0, keepdims=True)
    forward = [acc0[0:64, :CB] + acc1[0:64, :CB], acc0[64:128, :CB] + acc1[64:128, :CB]]
    reverse = [acc0[0:64, CB:] + acc1[128:192, CB:], acc0[128:192, CB:] + acc1[192:256, CB:]]
    forward0 = [total(acc0[192:200, :CB]) + total(acc1[256:264, :CB]), total(acc0[200:208, :CB]) + total(acc1[264:272, :CB])]
    reverse0 = [total(acc0[192:200, CB:]) + total(acc1[272:280, CB:]), total(acc0[208:216, CB:]) + total(acc1[280:288, CB:])]
    lag = lax.broadcasted_iota(jnp.int32, (CB, 64), 0)
    r = lax.broadcasted_iota(jnp.int32, (CB, 64), 1)
    m = (r >> 3) * 8 + 8 - (r & 7)
    to_forward = jnp.where(lag == m, 1.0, 0.0)
    to_reverse = jnp.where(lag == 64 - m, 1.0, 0.0)
    lag_row = lax.broadcasted_iota(jnp.int32, (CB, CB), 0)
    parts = []
    for q in range(2):
        exact = lambda s, v: lax.dot_general(s, v, NN, precision=lax.Precision.HIGHEST, preferred_element_type=F32)
        part = exact(to_forward, forward[q]) + exact(to_reverse, reverse[q])
        part = part + jnp.where(lag_row == 0, forward0[q], 0.0) + jnp.where(lag_row == 64, reverse0[q], 0.0)
        parts.append(part)
    out_ref[:, :CB] = jnp.transpose(parts[0] - parts[1])
    out_ref[:, CB:] = jnp.transpose(parts[1])


def fused(flags, scales, bins, stream, lower, upper, far, special, time_scale):
    return pl.pallas_call(
        functools.partial(fused_kernel, time_scale),
        in_specs=[SMEM] + [VMEM] * 7,
        out_specs=VMEM,
        out_shape=jax.ShapeDtypeStruct((CB, 2 * CB), F32),
        scratch_shapes=[pltpu.VMEM((3, CB, W), F32), pltpu.VMEM((3, 1024, W), BF),
                        pltpu.VMEM((2, 1024, W), BF), pltpu.VMEM((3, 1024, 1024), F32), pltpu.VMEM((3, CB, CB), F32),
                        pltpu.VMEM((3, CB, CB), F32), pltpu.VMEM((4, CB, CB), F32), pltpu.VMEM((4, CB, CB), F32),
                        pltpu.VMEM((224, 2 * CB), F32), pltpu.VMEM((288, 2 * CB), F32)],
        compiler_params=pltpu.CompilerParams(vmem_limit_bytes=36 << 20),
        cost_estimate=pl.CostEstimate(flops=4 * 2 * 1024 * 1024 * W, bytes_accessed=6 << 20, transcendentals=0),
        name="lags_and_bins",
    )(flags, scales, bins, stream, lower, upper, far, special)


MAX_LAG = 32
NB = 256
ROUNDS = 2
EPSILON = 1e-06
HALF = 1024


def payload_kernel(flags, squares, traces, bins, stream_ref, far_ref, upper_ref, special_ref, edge, bins_v, sems):
    high, first, last = (flags[i] == 1 for i in range(3))
    mine = pl.multiple_of(jnp.where(high, HALF, 0), HALF)
    other = pl.multiple_of(HALF - mine, HALF)
    upper_start = pl.multiple_of(jnp.where(first, other, mine), HALF)
    special_start = pl.multiple_of(jnp.where(last, other, mine), HALF)
    part = lambda start: traces.at[:, pl.ds(start, HALF)]
    main = pl.ds(0, HALF)
    copies = [pltpu.make_async_copy(traces.at[:, pl.ds(HALF - CB, 2 * CB)], edge, sems.at[0]),
              pltpu.make_async_copy(bins, bins_v, sems.at[1])]
    for n, (start, ref) in enumerate(((mine, stream_ref), (other, far_ref), (upper_start, upper_ref), (special_start, special_ref))):
        copies.append(pltpu.make_async_copy(part(start), ref.at[:, main], sems.at[2 + n]))
    for copy in copies:
        copy.start()
    lane = lax.broadcasted_iota(jnp.int32, (CB, CB), 1)
    none = jnp.zeros((CB, CB), F32)
    copies[0].wait()
    halo_low = jnp.where(lane < MAX_LAG, edge[:, CB:].astype(F32), none)
    halo_high = jnp.where(lane >= CB - MAX_LAG, edge[:, :CB].astype(F32), none)
    keep_low = jnp.where(high, 0.0, 1.0)
    keep_high = 1.0 - keep_low
    stream_ref[:, HALF:] = (halo_low * keep_low).astype(BF)
    upper_ref[:, HALF:W] = (halo_low * jnp.where(first, keep_high, keep_low)).astype(BF)
    far_ref[:, HALF:W] = (halo_high * keep_low).astype(BF)
    special_ref[:, HALF:] = (halo_high * jnp.where(last, keep_low, keep_high)).astype(BF)
    copies[1].wait()
    far_ref[:, W:W + CB] = bins_v[0].astype(F32).astype(BF)
    far_ref[:, W + CB:] = bins_v[1].astype(F32).astype(BF)
    upper_ref[:, W:] = bins_v[1].astype(F32).astype(BF)
    for copy in copies[2:]:
        copy.wait()


def payloads(flags, squares, traces, bins):
    return pl.pallas_call(
        payload_kernel,
        in_specs=[SMEM, VMEM, pl.BlockSpec(memory_space=pl.ANY), pl.BlockSpec(memory_space=pl.ANY)],
        out_specs=[VMEM] * 4,
        out_shape=[jax.ShapeDtypeStruct((CB, width), BF) for width in (W, W + 2 * CB, W + CB, W)],
        scratch_shapes=[pltpu.VMEM((CB, 2 * CB), BF), pltpu.VMEM((2, CB, CB), jnp.int32), pltpu.SemaphoreType.DMA((6,))],
        compiler_params=pltpu.CompilerParams(vmem_limit_bytes=8 << 20),
        cost_estimate=pl.CostEstimate(flops=1 << 18, bytes_accessed=2 << 20, transcendentals=0),
        name="payloads",
    )(flags, squares, traces, bins)


def square_kernel(traces, out_ref):
    total = jnp.zeros((CB, CB), F32)
    for t in range(2 * HALF // CB):
        x = traces[:, CB * t:CB * t + CB].astype(F32)
        total = total + x * x
    out_ref[...] = jnp.sum(jnp.transpose(total), axis=0, keepdims=True)


def square_sums(traces):
    return pl.pallas_call(
        square_kernel,
        in_specs=[VMEM],
        out_specs=VMEM,
        out_shape=jax.ShapeDtypeStruct((1, CB), F32),
        compiler_params=pltpu.CompilerParams(vmem_limit_bytes=4 << 20),
        cost_estimate=pl.CostEstimate(flops=1 << 18, bytes_accessed=1 << 19, transcendentals=0),
        name="square_sums",
    )(traces)


def copies_kernel(*refs):
    rows = jnp.concatenate([ref[...] for ref in refs[:-1]], 0)
    refs[-1][...] = jnp.broadcast_to(rows[None], refs[-1].shape)


def copies_of(rows, count):
    return pl.pallas_call(
        copies_kernel,
        in_specs=[VMEM] * len(rows),
        out_specs=VMEM,
        out_shape=jax.ShapeDtypeStruct((count, len(rows), CB), F32),
        compiler_params=pltpu.CompilerParams(vmem_limit_bytes=2 << 20),
        cost_estimate=pl.CostEstimate(flops=1 << 12, bytes_accessed=1 << 15, transcendentals=0),
        name="square_copies",
    )(*rows)


def inverse_rms_kernel(total_time, gathered, out_ref):
    out_ref[...] = lax.rsqrt(jnp.sum(gathered[...], axis=0) / total_time + EPSILON)


def inverse_rms(gathered, total_time):
    return pl.pallas_call(
        functools.partial(inverse_rms_kernel, total_time),
        in_specs=[VMEM],
        out_specs=VMEM,
        out_shape=jax.ShapeDtypeStruct((4, CB), F32),
        compiler_params=pltpu.CompilerParams(vmem_limit_bytes=2 << 20),
        cost_estimate=pl.CostEstimate(flops=1 << 12, bytes_accessed=1 << 13, transcendentals=0),
        name="inverse_rms",
    )(gathered)


def exchange(block, source):
    n = lax.axis_size("chan")
    return lax.ppermute(block, "chan", [(source(i), i) for i in range(n)])


FAR = lambda i: i ^ 8
LOWER = lambda i: (i & 8) | ((i - 1) & 7)
UPPER = lambda i: (i & 8) | ((i + 1) & 7)


def local(traces, pair_bins):
    total_time = traces.shape[1] * lax.axis_size("seg")
    chan_count, seg_count = lax.axis_size("chan"), lax.axis_size("seg")
    index = lax.axis_index("chan")
    depth = index % 8
    flags = jnp.stack([index // 8, (depth == 0).astype(jnp.int32), (depth == 7).astype(jnp.int32)])
    squares = square_sums(traces)
    stream, far_payload, upper_payload, special = payloads(flags, squares, traces, pair_bins)
    with jax.named_scope("send_squares"):
        rows = [squares] + [exchange(squares, source) for source in (FAR, LOWER, UPPER)]
    rows, stream, far_payload, upper_payload = lax.optimization_barrier((rows, stream, far_payload, upper_payload))
    with jax.named_scope("send_blocks"):
        far = exchange(far_payload, FAR)
        lower = exchange(stream, LOWER)
        upper = exchange(upper_payload, UPPER)
    with jax.named_scope("energies"):
        gathered = lax.all_to_all(copies_of(rows, seg_count), "seg", 0, 0, tiled=True)
        scales = inverse_rms(gathered, total_time)
    partial_stack = fused(flags, scales, pair_bins, stream, lower, upper, far, special,
                          1.0 / math.sqrt(total_time))
    with jax.named_scope("reduce_bins"):
        slots = partial_stack.reshape(chan_count, CB // chan_count, 2 * CB)
        owned = jnp.sum(lax.all_to_all(slots, "chan", 0, 0, tiled=True), axis=0)
        copies = jnp.broadcast_to(owned[None], (seg_count,) + owned.shape)
        owned = jnp.sum(lax.all_to_all(copies, "seg", 0, 0, tiled=True), axis=0)
    pair_total = ROUNDS * chan_count * CB * CB // NB
    owned = owned.reshape(-1, 2, CB)[:, :, :2 * MAX_LAG + 1] * (1.0 / math.sqrt(pair_total))
    return jnp.transpose(owned, (2, 0, 1)).reshape(2 * MAX_LAG + 1, -1)


def solution(mesh):
    in_specs = (P("chan", "seg"), P(None, "chan", None))
    out_specs = P(None, "chan")
    return jax.shard_map(local, mesh=mesh, in_specs=in_specs, out_specs=out_specs, check_vma=False)
```

```python
import functools
import math

import jax
import jax.numpy as jnp
from jax import lax
from jax.experimental import pallas as pl
from jax.experimental.pallas import tpu as pltpu
from jax.sharding import PartitionSpec as P

NT = (((1,), (1,)), ((), ()))
NN = (((1,), (0,)), ((), ()))
F32, BF = jnp.float32, jnp.bfloat16
W = 1152
CB = 128
VMEM = pl.BlockSpec(memory_space=pltpu.VMEM)
SMEM = pl.BlockSpec(memory_space=pltpu.SMEM)


def lag_rows(ref, start, count):
    rows = []
    for ii in range(count):
        x = jnp.broadcast_to(ref[pl.ds(start + ii, 1), :], (8, W))
        rows.append(pltpu.roll(x, 24, 1, stride=1, stride_axis=0))
    return jnp.concatenate(rows, 0).astype(BF)


def shift_rows(block, out_ref):
    for p in range(8):
        out_ref[CB * p:CB * p + CB, :] = block if p == 0 else pltpu.roll(block, 8 * p, 1)


GROUP = 8
STEP = 64


def fused_kernel(time_scale, flags, scale_ref, bins_ref, stream, lower, upper, far, special, out_ref,
                 wide, lags, shifted, c_first, c_ref, c0_ref, pair_scale, hi, lo, acc0, acc1):
    shift_rows(far[:, :W], shifted.at[0])
    wide[0] = stream[...].astype(F32)
    wide[1] = lower[...].astype(F32)
    wide[2] = upper[:, :W].astype(F32)
    iota = lax.broadcasted_iota(jnp.int32, (CB, CB), 0).astype(F32).astype(BF)
    one, zero = jnp.ones((CB, CB), BF), jnp.zeros((CB, CB), BF)
    sub = lax.broadcasted_iota(jnp.int32, (32, CB), 0) & 7
    slots = (0, flags[1], flags[2])

    def zscore(k, i, local):
        rows = c_first[pl.ds(pl.multiple_of(i * 8, 8), 8), :] if k == 0 else c_ref[k - 1, 8 * local:8 * local + 8, :]
        z = jnp.concatenate([rows[:, CB * p:CB * p + CB] for p in range(8)], 0)
        return (z * pair_scale[k, pl.ds(i, 1), :]).astype(BF)

    def low(t, i):
        return jnp.broadcast_to(lo[t, pl.ds(i, 1), :], (64, CB)).astype(BF)

    def onehot(t, i):
        return jnp.where(jnp.broadcast_to(hi[t, pl.ds(i, 1), :], (CB, CB)).astype(BF) == iota, one, zero)

    def bin_group(start, g):
        base = pl.multiple_of(start + g * GROUP, GROUP)
        rows = pl.ds(base, GROUP)
        x = [c0_ref[k, rows, :] * pair_scale[k, rows, :] for k in range(3)]
        low8 = [lo[t, rows, :] for t in range(4)]
        extra0 = jnp.concatenate([x[0], x[0] * low8[0], x[0] * low8[1], jnp.zeros_like(x[0])], 0)
        extra1 = jnp.concatenate([x[1], x[1] * low8[2], x[2], x[2] * low8[3]], 0)
        left0, left1, right0, right1 = [], [], [], []
        for ii in range(GROUP):
            i = base + ii
            e0 = jnp.where(sub == ii, extra0, 0.0).astype(BF)
            e1 = jnp.where(sub == ii, extra1, 0.0).astype(BF)
            z = [zscore(k, i, g * GROUP + ii) for k in range(3)]
            left0.append(jnp.concatenate([z[0], z[0] * low(0, i), z[0] * low(1, i), e0], 0))
            left1.append(jnp.concatenate([z[1], z[1] * low(2, i), z[2], z[2] * low(3, i), e1], 0))
            right0.append(jnp.concatenate([onehot(0, i), onehot(1, i)], 0))
            right1.append(jnp.concatenate([onehot(2, i), onehot(3, i)], 0))
        cat = lambda blocks: jnp.concatenate(blocks, 1)
        acc0[...] += lax.dot_general(cat(left0), cat(right0), NT, preferred_element_type=F32)
        acc1[...] += lax.dot_general(cat(left1), cat(right1), NT, preferred_element_type=F32)

    def prepare():
        first, last = flags[1] == 1, flags[2] == 1
        own, far_scale = scale_ref[0:1, :], scale_ref[1:2, :]
        held = (far_scale, jnp.where(first, own, far_scale), jnp.where(last, own, far_scale))
        for t, streamed in enumerate((own, scale_ref[2:3, :], scale_ref[3:4, :])):
            column = jnp.transpose(jnp.broadcast_to(streamed, (CB, CB)))
            pair_scale[t] = column * (held[t] * time_scale)
        sets = (far[:, W:W + CB].astype(F32), bins_ref[0].astype(F32),
                jnp.where(first, bins_ref[1].astype(F32), far[:, W + CB:].astype(F32)), upper[:, W:].astype(F32))
        for t, b in enumerate(sets):
            if t % 2 == 0:
                b = jnp.transpose(b)
            owner = jnp.floor(b * (1.0 / 16.0))
            rest = b - 16.0 * owner
            high_half = jnp.where(rest >= 8.0, 1.0, 0.0)
            hi[t] = 8.0 * owner + rest - 8.0 * high_half
            lo[t] = high_half
        acc0[...] = jnp.zeros_like(acc0)
        acc1[...] = jnp.zeros_like(acc1)
        ahead = jnp.concatenate([pltpu.roll(far[:, :W], W - 32, 1), pltpu.roll(special[...], W - 32, 1)], 0)
        for k, block in enumerate((stream[...], lower[...], upper[:, :W])):
            pair = lax.dot_general(block, ahead, NT, preferred_element_type=F32)
            c0_ref[k] = pair[:, :CB] if k == 0 else jnp.where(flags[k] == 1, pair[:, CB:], pair[:, :CB])

    lag_a, lag_b, lag_c = (lags.at[k] for k in range(3))
    half = 8 * STEP
    lag_a[...] = lag_rows(wide.at[0], 0, STEP)
    c_first[:half, :] = lax.dot_general(lag_a[...], shifted[0], NT, preferred_element_type=F32)
    shift_rows(special[...], shifted.at[1])
    lag_c[...] = lag_rows(wide.at[0], STEP, STEP)
    c_first[half:, :] = lax.dot_general(lag_c[...], shifted[0], NT, preferred_element_type=F32)
    prepare()
    lag_b[...] = lag_rows(wide.at[1], 0, STEP)

    def chunk(m, carry):
        start = m * STEP
        c_ref[0] = lax.dot_general(lag_b[...], shifted[slots[1]], NT, preferred_element_type=F32)
        lag_c[...] = lag_rows(wide.at[2], start, STEP)
        c_ref[1] = lax.dot_general(lag_c[...], shifted[slots[2]], NT, preferred_element_type=F32)
        lag_b[...] = lag_rows(wide.at[1], lax.rem(start + STEP, CB), STEP)
        for g in range(STEP // GROUP):
            bin_group(start, g)
        return carry

    lax.fori_loop(0, CB // STEP, chunk, 0)

    total = lambda v: jnp.sum(v, axis=0, keepdims=True)
    forward = [acc0[0:64, :CB] + acc1[0:64, :CB], acc0[64:128, :CB] + acc1[64:128, :CB]]
    reverse = [acc0[0:64, CB:] + acc1[128:192, CB:], acc0[128:192, CB:] + acc1[192:256, CB:]]
    forward0 = [total(acc0[192:200, :CB]) + total(acc1[256:264, :CB]), total(acc0[200:208, :CB]) + total(acc1[264:272, :CB])]
    reverse0 = [total(acc0[192:200, CB:]) + total(acc1[272:280, CB:]), total(acc0[208:216, CB:]) + total(acc1[280:288, CB:])]
    lag = lax.broadcasted_iota(jnp.int32, (CB, CB), 0)
    c = lax.broadcasted_iota(jnp.int32, (CB, CB), 1)
    r = c & 63
    m = (r >> 3) * 8 + 8 - (r & 7)
    place = jnp.where(lag == jnp.where(c < 64, m, 64 - m), 1.0, 0.0).astype(BF)
    rest = jnp.concatenate([jnp.concatenate([forward[q], reverse[q]], 0) for q in range(2)], 1)
    both = jnp.zeros((CB, 2 * CB), F32)
    for _piece in range(3):
        piece = rest.astype(BF)
        rest = rest - piece.astype(F32)
        both = both + lax.dot_general(place, piece, NN, preferred_element_type=F32)
    parts = [both[:, q * CB:q * CB + CB] + jnp.where(lag == 0, forward0[q], 0.0) + jnp.where(lag == 64, reverse0[q], 0.0)
             for q in range(2)]
    out_ref[:, :CB] = jnp.transpose(parts[0] - parts[1])
    out_ref[:, CB:] = jnp.transpose(parts[1])


def fused(flags, scales, bins, stream, lower, upper, far, special, time_scale):
    return pl.pallas_call(
        functools.partial(fused_kernel, time_scale),
        in_specs=[SMEM] + [VMEM] * 7,
        out_specs=VMEM,
        out_shape=jax.ShapeDtypeStruct((CB, 2 * CB), F32),
        scratch_shapes=[pltpu.VMEM((3, CB, W), F32), pltpu.VMEM((3, 8 * STEP, W), BF),
                        pltpu.VMEM((2, 1024, W), BF), pltpu.VMEM((1024, 1024), F32), pltpu.VMEM((2, 8 * STEP, 1024), F32), pltpu.VMEM((3, CB, CB), F32),
                        pltpu.VMEM((3, CB, CB), F32), pltpu.VMEM((4, CB, CB), F32), pltpu.VMEM((4, CB, CB), F32),
                        pltpu.VMEM((224, 2 * CB), F32), pltpu.VMEM((288, 2 * CB), F32)],
        compiler_params=pltpu.CompilerParams(vmem_limit_bytes=36 << 20),
        cost_estimate=pl.CostEstimate(flops=4 * 2 * 1024 * 1024 * W, bytes_accessed=6 << 20, transcendentals=0),
        name="lags_and_bins",
    )(flags, scales, bins, stream, lower, upper, far, special)


MAX_LAG = 32
NB = 256
ROUNDS = 2
EPSILON = 1e-06
HALF = 1024


def payload_kernel(flags, squares, traces, bins, stream_ref, far_ref, upper_ref, special_ref, edge, bins_v, sems):
    high, first, last = (flags[i] == 1 for i in range(3))
    mine = pl.multiple_of(jnp.where(high, HALF, 0), HALF)
    other = pl.multiple_of(HALF - mine, HALF)
    upper_start = pl.multiple_of(jnp.where(first, other, mine), HALF)
    special_start = pl.multiple_of(jnp.where(last, other, mine), HALF)
    part = lambda start: traces.at[:, pl.ds(start, HALF)]
    main = pl.ds(0, HALF)
    copies = [pltpu.make_async_copy(traces.at[:, pl.ds(HALF - CB, 2 * CB)], edge, sems.at[0]),
              pltpu.make_async_copy(bins, bins_v, sems.at[1])]
    for n, (start, ref) in enumerate(((mine, stream_ref), (other, far_ref), (upper_start, upper_ref), (special_start, special_ref))):
        copies.append(pltpu.make_async_copy(part(start), ref.at[:, main], sems.at[2 + n]))
    for copy in copies:
        copy.start()
    lane = lax.broadcasted_iota(jnp.int32, (CB, CB), 1)
    none = jnp.zeros((CB, CB), F32)
    copies[0].wait()
    halo_low = jnp.where(lane < MAX_LAG, edge[:, CB:].astype(F32), none)
    halo_high = jnp.where(lane >= CB - MAX_LAG, edge[:, :CB].astype(F32), none)
    keep_low = jnp.where(high, 0.0, 1.0)
    keep_high = 1.0 - keep_low
    stream_ref[:, HALF:] = (halo_low * keep_low).astype(BF)
    upper_ref[:, HALF:W] = (halo_low * jnp.where(first, keep_high, keep_low)).astype(BF)
    far_ref[:, HALF:W] = (halo_high * keep_low).astype(BF)
    special_ref[:, HALF:] = (halo_high * jnp.where(last, keep_low, keep_high)).astype(BF)
    copies[1].wait()
    far_ref[:, W:W + CB] = bins_v[0].astype(F32).astype(BF)
    far_ref[:, W + CB:] = bins_v[1].astype(F32).astype(BF)
    upper_ref[:, W:] = bins_v[1].astype(F32).astype(BF)
    for copy in copies[2:]:
        copy.wait()


def payloads(flags, squares, traces, bins):
    return pl.pallas_call(
        payload_kernel,
        in_specs=[SMEM, VMEM, pl.BlockSpec(memory_space=pl.ANY), pl.BlockSpec(memory_space=pl.ANY)],
        out_specs=[VMEM] * 4,
        out_shape=[jax.ShapeDtypeStruct((CB, width), BF) for width in (W, W + 2 * CB, W + CB, W)],
        scratch_shapes=[pltpu.VMEM((CB, 2 * CB), BF), pltpu.VMEM((2, CB, CB), jnp.int32), pltpu.SemaphoreType.DMA((6,))],
        compiler_params=pltpu.CompilerParams(vmem_limit_bytes=8 << 20),
        cost_estimate=pl.CostEstimate(flops=1 << 18, bytes_accessed=2 << 20, transcendentals=0),
        name="payloads",
    )(flags, squares, traces, bins)


def square_kernel(traces, out_ref):
    total = jnp.zeros((CB, CB), F32)
    for t in range(2 * HALF // CB):
        x = traces[:, CB * t:CB * t + CB].astype(F32)
        total = total + x * x
    out_ref[...] = jnp.sum(jnp.transpose(total), axis=0, keepdims=True)


def square_sums(traces):
    return pl.pallas_call(
        square_kernel,
        in_specs=[VMEM],
        out_specs=VMEM,
        out_shape=jax.ShapeDtypeStruct((1, CB), F32),
        compiler_params=pltpu.CompilerParams(vmem_limit_bytes=4 << 20),
        cost_estimate=pl.CostEstimate(flops=1 << 18, bytes_accessed=1 << 19, transcendentals=0),
        name="square_sums",
    )(traces)


def copies_kernel(*refs):
    rows = jnp.concatenate([ref[...] for ref in refs[:-1]], 0)
    refs[-1][...] = jnp.broadcast_to(rows[None], refs[-1].shape)


def copies_of(rows, count):
    return pl.pallas_call(
        copies_kernel,
        in_specs=[VMEM] * len(rows),
        out_specs=VMEM,
        out_shape=jax.ShapeDtypeStruct((count, len(rows), CB), F32),
        compiler_params=pltpu.CompilerParams(vmem_limit_bytes=2 << 20),
        cost_estimate=pl.CostEstimate(flops=1 << 12, bytes_accessed=1 << 15, transcendentals=0),
        name="square_copies",
    )(*rows)


def inverse_rms_kernel(total_time, gathered, out_ref):
    out_ref[...] = lax.rsqrt(jnp.sum(gathered[...], axis=0) / total_time + EPSILON)


def inverse_rms(gathered, total_time):
    return pl.pallas_call(
        functools.partial(inverse_rms_kernel, total_time),
        in_specs=[VMEM],
        out_specs=VMEM,
        out_shape=jax.ShapeDtypeStruct((4, CB), F32),
        compiler_params=pltpu.CompilerParams(vmem_limit_bytes=2 << 20),
        cost_estimate=pl.CostEstimate(flops=1 << 12, bytes_accessed=1 << 13, transcendentals=0),
        name="inverse_rms",
    )(gathered)


def finish_kernel(scale, gathered, out_ref):
    total = jnp.sum(gathered[...], axis=0) * scale
    rows = jnp.concatenate([total[:, :CB], total[:, CB:]], 0)
    out_ref[...] = jnp.transpose(rows)[:2 * MAX_LAG + 1, :]


def finish(gathered, scale):
    return pl.pallas_call(
        functools.partial(finish_kernel, scale),
        in_specs=[VMEM],
        out_specs=VMEM,
        out_shape=jax.ShapeDtypeStruct((2 * MAX_LAG + 1, 2 * gathered.shape[1]), F32),
        compiler_params=pltpu.CompilerParams(vmem_limit_bytes=2 << 20),
        cost_estimate=pl.CostEstimate(flops=1 << 15, bytes_accessed=1 << 17, transcendentals=0),
        name="finish",
    )(gathered)


def exchange(block, source):
    n = lax.axis_size("chan")
    return lax.ppermute(block, "chan", [(source(i), i) for i in range(n)])


FAR = lambda i: i ^ 8
LOWER = lambda i: (i & 8) | ((i - 1) & 7)
UPPER = lambda i: (i & 8) | ((i + 1) & 7)


def local(traces, pair_bins):
    total_time = traces.shape[1] * lax.axis_size("seg")
    chan_count, seg_count = lax.axis_size("chan"), lax.axis_size("seg")
    index = lax.axis_index("chan")
    depth = index % 8
    flags = jnp.stack([index // 8, (depth == 0).astype(jnp.int32), (depth == 7).astype(jnp.int32)])
    squares = square_sums(traces)
    stream, far_payload, upper_payload, special = payloads(flags, squares, traces, pair_bins)
    with jax.named_scope("send_squares"):
        rows = [squares] + [exchange(squares, source) for source in (FAR, LOWER, UPPER)]
    rows, stream, far_payload, upper_payload = lax.optimization_barrier((rows, stream, far_payload, upper_payload))
    with jax.named_scope("send_blocks"):
        far = exchange(far_payload, FAR)
        lower = exchange(stream, LOWER)
        upper = exchange(upper_payload, UPPER)
    with jax.named_scope("energies"):
        gathered = lax.all_to_all(copies_of(rows, seg_count), "seg", 0, 0, tiled=True)
        scales = inverse_rms(gathered, total_time)
    partial_stack = fused(flags, scales, pair_bins, stream, lower, upper, far, special,
                          1.0 / math.sqrt(total_time))
    with jax.named_scope("reduce_bins"):
        slots = partial_stack.reshape(chan_count, CB // chan_count, 2 * CB)
        owned = jnp.sum(lax.all_to_all(slots, "chan", 0, 0, tiled=True), axis=0)
        copies = jnp.broadcast_to(owned[None], (seg_count,) + owned.shape)
        gathered = lax.all_to_all(copies, "seg", 0, 0, tiled=True)
        pair_total = ROUNDS * chan_count * CB * CB // NB
        return finish(gathered, 1.0 / math.sqrt(pair_total))


def solution(mesh):
    in_specs = (P("chan", "seg"), P(None, "chan", None))
    out_specs = P(None, "chan")
    return jax.shard_map(local, mesh=mesh, in_specs=in_specs, out_specs=out_specs, check_vma=False)
```

```python
import functools
import math

import jax
import jax.numpy as jnp
from jax import lax
from jax.experimental import pallas as pl
from jax.experimental.pallas import tpu as pltpu
from jax.sharding import PartitionSpec as P

NT = (((1,), (1,)), ((), ()))
NN = (((1,), (0,)), ((), ()))
F32, BF = jnp.float32, jnp.bfloat16
W = 1152
CB = 128
VMEM = pl.BlockSpec(memory_space=pltpu.VMEM)
SMEM = pl.BlockSpec(memory_space=pltpu.SMEM)


def lag_rows(ref, start, count):
    rows = []
    for ii in range(count):
        x = jnp.broadcast_to(ref[pl.ds(start + ii, 1), :], (8, W))
        rows.append(pltpu.roll(x, 24, 1, stride=1, stride_axis=0))
    return jnp.concatenate(rows, 0).astype(BF)


def shift_rows(block, out_ref):
    for p in range(8):
        out_ref[CB * p:CB * p + CB, :] = block if p == 0 else pltpu.roll(block, 8 * p, 1)


GROUP = 8
STEP = 64


def fused_kernel(time_scale, flags, scale_ref, bins_ref, stream, lower, upper, far, special, out_ref,
                 wide, lags, shifted, c_first, c_ref, c0_ref, pair_scale, hi, lo, acc0, acc1):
    shift_rows(far[:, :W], shifted.at[0])
    wide[0] = stream[...].astype(F32)
    wide[1] = lower[...].astype(F32)
    wide[2] = upper[:, :W].astype(F32)
    iota = lax.broadcasted_iota(jnp.int32, (CB, CB), 0).astype(F32).astype(BF)
    one, zero = jnp.ones((CB, CB), BF), jnp.zeros((CB, CB), BF)
    sub = lax.broadcasted_iota(jnp.int32, (32, CB), 0) & 7
    slots = (0, flags[1], flags[2])

    def zscore(k, i, local):
        rows = c_first[pl.ds(pl.multiple_of(i * 8, 8), 8), :] if k == 0 else c_ref[k - 1, 8 * local:8 * local + 8, :]
        z = jnp.concatenate([rows[:, CB * p:CB * p + CB] for p in range(8)], 0)
        return (z * pair_scale[k, pl.ds(i, 1), :]).astype(BF)

    def low(t, i):
        return jnp.broadcast_to(lo[t, pl.ds(i, 1), :], (64, CB)).astype(BF)

    def onehot(t, i):
        return jnp.where(jnp.broadcast_to(hi[t, pl.ds(i, 1), :], (CB, CB)).astype(BF) == iota, one, zero)

    def bin_group(start, g):
        base = pl.multiple_of(start + g * GROUP, GROUP)
        rows = pl.ds(base, GROUP)
        x = [c0_ref[k, rows, :] * pair_scale[k, rows, :] for k in range(3)]
        low8 = [lo[t, rows, :] for t in range(4)]
        extra0 = jnp.concatenate([x[0], x[0] * low8[0], x[0] * low8[1], jnp.zeros_like(x[0])], 0)
        extra1 = jnp.concatenate([x[1], x[1] * low8[2], x[2], x[2] * low8[3]], 0)
        left0, left1, right0, right1 = [], [], [], []
        for ii in range(GROUP):
            i = base + ii
            e0 = jnp.where(sub == ii, extra0, 0.0).astype(BF)
            e1 = jnp.where(sub == ii, extra1, 0.0).astype(BF)
            z = [zscore(k, i, g * GROUP + ii) for k in range(3)]
            left0.append(jnp.concatenate([z[0], z[0] * low(0, i), z[0] * low(1, i), e0], 0))
            left1.append(jnp.concatenate([z[1], z[1] * low(2, i), z[2], z[2] * low(3, i), e1], 0))
            right0.append(jnp.concatenate([onehot(0, i), onehot(1, i)], 0))
            right1.append(jnp.concatenate([onehot(2, i), onehot(3, i)], 0))
        cat = lambda blocks: jnp.concatenate(blocks, 1)
        acc0[...] += lax.dot_general(cat(left0), cat(right0), NT, preferred_element_type=F32)
        acc1[...] += lax.dot_general(cat(left1), cat(right1), NT, preferred_element_type=F32)

    def prepare():
        first, last = flags[1] == 1, flags[2] == 1
        own, far_scale = scale_ref[0:1, :], scale_ref[1:2, :]
        held = (far_scale, jnp.where(first, own, far_scale), jnp.where(last, own, far_scale))
        for t, streamed in enumerate((own, scale_ref[2:3, :], scale_ref[3:4, :])):
            column = jnp.transpose(jnp.broadcast_to(streamed, (CB, CB)))
            pair_scale[t] = column * (held[t] * time_scale)
        sets = (far[:, W:W + CB].astype(F32), bins_ref[0].astype(F32),
                jnp.where(first, bins_ref[1].astype(F32), far[:, W + CB:].astype(F32)), upper[:, W:].astype(F32))
        for t, b in enumerate(sets):
            if t % 2 == 0:
                b = jnp.transpose(b)
            owner = jnp.floor(b * (1.0 / 16.0))
            rest = b - 16.0 * owner
            high_half = jnp.where(rest >= 8.0, 1.0, 0.0)
            hi[t] = 8.0 * owner + rest - 8.0 * high_half
            lo[t] = high_half
        acc0[...] = jnp.zeros_like(acc0)
        acc1[...] = jnp.zeros_like(acc1)
        ahead = jnp.concatenate([pltpu.roll(far[:, :W], W - 32, 1), pltpu.roll(special[...], W - 32, 1)], 0)
        for k, block in enumerate((stream[...], lower[...], upper[:, :W])):
            pair = lax.dot_general(block, ahead, NT, preferred_element_type=F32)
            c0_ref[k] = pair[:, :CB] if k == 0 else jnp.where(flags[k] == 1, pair[:, CB:], pair[:, :CB])

    lag_a, lag_b, lag_c = (lags.at[k] for k in range(3))
    half = 8 * STEP
    lag_a[...] = lag_rows(wide.at[0], 0, STEP)
    c_first[:half, :] = lax.dot_general(lag_a[...], shifted[0], NT, preferred_element_type=F32)
    shift_rows(special[...], shifted.at[1])
    lag_c[...] = lag_rows(wide.at[0], STEP, STEP)
    c_first[half:, :] = lax.dot_general(lag_c[...], shifted[0], NT, preferred_element_type=F32)
    prepare()
    lag_b[...] = lag_rows(wide.at[1], 0, STEP)

    def chunk(m, carry):
        start = m * STEP
        c_ref[0] = lax.dot_general(lag_b[...], shifted[slots[1]], NT, preferred_element_type=F32)
        lag_c[...] = lag_rows(wide.at[2], start, STEP)
        c_ref[1] = lax.dot_general(lag_c[...], shifted[slots[2]], NT, preferred_element_type=F32)
        lag_b[...] = lag_rows(wide.at[1], lax.rem(start + STEP, CB), STEP)
        for g in range(STEP // GROUP):
            bin_group(start, g)
        return carry

    lax.fori_loop(0, CB // STEP, chunk, 0)

    total = lambda v: jnp.sum(v, axis=0, keepdims=True)
    forward = [acc0[0:64, :CB] + acc1[0:64, :CB], acc0[64:128, :CB] + acc1[64:128, :CB]]
    reverse = [acc0[0:64, CB:] + acc1[128:192, CB:], acc0[128:192, CB:] + acc1[192:256, CB:]]
    forward0 = [total(acc0[192:200, :CB]) + total(acc1[256:264, :CB]), total(acc0[200:208, :CB]) + total(acc1[264:272, :CB])]
    reverse0 = [total(acc0[192:200, CB:]) + total(acc1[272:280, CB:]), total(acc0[208:216, CB:]) + total(acc1[280:288, CB:])]
    lag = lax.broadcasted_iota(jnp.int32, (CB, CB), 0)
    c = lax.broadcasted_iota(jnp.int32, (CB, CB), 1)
    r = c & 63
    m = (r >> 3) * 8 + 8 - (r & 7)
    place = jnp.where(lag == jnp.where(c < 64, m, 64 - m), 1.0, 0.0).astype(BF)
    rest = jnp.concatenate([jnp.concatenate([forward[q], reverse[q]], 0) for q in range(2)], 1)
    both = jnp.zeros((CB, 2 * CB), F32)
    for _piece in range(3):
        piece = rest.astype(BF)
        rest = rest - piece.astype(F32)
        both = both + lax.dot_general(place, piece, NN, preferred_element_type=F32)
    parts = [both[:, q * CB:q * CB + CB] + jnp.where(lag == 0, forward0[q], 0.0) + jnp.where(lag == 64, reverse0[q], 0.0)
             for q in range(2)]
    out_ref[:, :CB] = jnp.transpose(parts[0] - parts[1])
    out_ref[:, CB:] = jnp.transpose(parts[1])


def fused(flags, scales, bins, stream, lower, upper, far, special, time_scale):
    return pl.pallas_call(
        functools.partial(fused_kernel, time_scale),
        in_specs=[SMEM] + [VMEM] * 7,
        out_specs=VMEM,
        out_shape=jax.ShapeDtypeStruct((CB, 2 * CB), F32),
        scratch_shapes=[pltpu.VMEM((3, CB, W), F32), pltpu.VMEM((3, 8 * STEP, W), BF),
                        pltpu.VMEM((2, 1024, W), BF), pltpu.VMEM((1024, 1024), F32), pltpu.VMEM((2, 8 * STEP, 1024), F32), pltpu.VMEM((3, CB, CB), F32),
                        pltpu.VMEM((3, CB, CB), F32), pltpu.VMEM((4, CB, CB), F32), pltpu.VMEM((4, CB, CB), F32),
                        pltpu.VMEM((224, 2 * CB), F32), pltpu.VMEM((288, 2 * CB), F32)],
        compiler_params=pltpu.CompilerParams(vmem_limit_bytes=36 << 20),
        cost_estimate=pl.CostEstimate(flops=4 * 2 * 1024 * 1024 * W, bytes_accessed=6 << 20, transcendentals=0),
        name="lags_and_bins",
    )(flags, scales, bins, stream, lower, upper, far, special)


MAX_LAG = 32
NB = 256
ROUNDS = 2
EPSILON = 1e-06
HALF = 1024


def payload_kernel(flags, squares, traces, bins, stream_ref, far_ref, upper_ref, special_ref, edge, bins_v, sems):
    high, first, last = (flags[i] == 1 for i in range(3))
    mine = pl.multiple_of(jnp.where(high, HALF, 0), HALF)
    other = pl.multiple_of(HALF - mine, HALF)
    upper_start = pl.multiple_of(jnp.where(first, other, mine), HALF)
    special_start = pl.multiple_of(jnp.where(last, other, mine), HALF)
    part = lambda start: traces.at[:, pl.ds(start, HALF)]
    main = pl.ds(0, HALF)
    copies = [pltpu.make_async_copy(traces.at[:, pl.ds(HALF - CB, 2 * CB)], edge, sems.at[0]),
              pltpu.make_async_copy(bins, bins_v, sems.at[1])]
    for n, (start, ref) in enumerate(((mine, stream_ref), (other, far_ref), (upper_start, upper_ref), (special_start, special_ref))):
        copies.append(pltpu.make_async_copy(part(start), ref.at[:, main], sems.at[2 + n]))
    for copy in copies:
        copy.start()
    lane = lax.broadcasted_iota(jnp.int32, (CB, CB), 1)
    none = jnp.zeros((CB, CB), F32)
    copies[0].wait()
    halo_low = jnp.where(lane < MAX_LAG, edge[:, CB:].astype(F32), none)
    halo_high = jnp.where(lane >= CB - MAX_LAG, edge[:, :CB].astype(F32), none)
    keep_low = jnp.where(high, 0.0, 1.0)
    keep_high = 1.0 - keep_low
    stream_ref[:, HALF:] = (halo_low * keep_low).astype(BF)
    upper_ref[:, HALF:W] = (halo_low * jnp.where(first, keep_high, keep_low)).astype(BF)
    far_ref[:, HALF:W] = (halo_high * keep_low).astype(BF)
    special_ref[:, HALF:] = (halo_high * jnp.where(last, keep_low, keep_high)).astype(BF)
    copies[1].wait()
    far_ref[:, W:W + CB] = bins_v[0].astype(F32).astype(BF)
    far_ref[:, W + CB:] = bins_v[1].astype(F32).astype(BF)
    upper_ref[:, W:] = bins_v[1].astype(F32).astype(BF)
    for copy in copies[2:]:
        copy.wait()


def payloads(flags, squares, traces, bins):
    return pl.pallas_call(
        payload_kernel,
        in_specs=[SMEM, VMEM, pl.BlockSpec(memory_space=pl.ANY), pl.BlockSpec(memory_space=pl.ANY)],
        out_specs=[VMEM] * 4,
        out_shape=[jax.ShapeDtypeStruct((CB, width), BF) for width in (W, W + 2 * CB, W + CB, W)],
        scratch_shapes=[pltpu.VMEM((CB, 2 * CB), BF), pltpu.VMEM((2, CB, CB), jnp.int32), pltpu.SemaphoreType.DMA((6,))],
        compiler_params=pltpu.CompilerParams(vmem_limit_bytes=8 << 20),
        cost_estimate=pl.CostEstimate(flops=1 << 18, bytes_accessed=2 << 20, transcendentals=0),
        name="payloads",
    )(flags, squares, traces, bins)


def square_kernel(traces, out_ref):
    total = jnp.zeros((CB, CB), F32)
    for t in range(2 * HALF // CB):
        x = traces[:, CB * t:CB * t + CB].astype(F32)
        total = total + x * x
    out_ref[...] = jnp.sum(jnp.transpose(total), axis=0, keepdims=True)


def square_sums(traces):
    return pl.pallas_call(
        square_kernel,
        in_specs=[VMEM],
        out_specs=VMEM,
        out_shape=jax.ShapeDtypeStruct((1, CB), F32),
        compiler_params=pltpu.CompilerParams(vmem_limit_bytes=4 << 20),
        cost_estimate=pl.CostEstimate(flops=1 << 18, bytes_accessed=1 << 19, transcendentals=0),
        name="square_sums",
    )(traces)


def copies_kernel(*refs):
    rows = jnp.concatenate([ref[...] for ref in refs[:-1]], 0)
    refs[-1][...] = jnp.broadcast_to(rows[None], refs[-1].shape)


def copies_of(rows, count):
    return pl.pallas_call(
        copies_kernel,
        in_specs=[VMEM] * len(rows),
        out_specs=VMEM,
        out_shape=jax.ShapeDtypeStruct((count, len(rows), CB), F32),
        compiler_params=pltpu.CompilerParams(vmem_limit_bytes=2 << 20),
        cost_estimate=pl.CostEstimate(flops=1 << 12, bytes_accessed=1 << 15, transcendentals=0),
        name="square_copies",
    )(*rows)


def inverse_rms_kernel(total_time, gathered, out_ref):
    out_ref[...] = lax.rsqrt(jnp.sum(gathered[...], axis=0) / total_time + EPSILON)


def inverse_rms(gathered, total_time):
    return pl.pallas_call(
        functools.partial(inverse_rms_kernel, total_time),
        in_specs=[VMEM],
        out_specs=VMEM,
        out_shape=jax.ShapeDtypeStruct((4, CB), F32),
        compiler_params=pltpu.CompilerParams(vmem_limit_bytes=2 << 20),
        cost_estimate=pl.CostEstimate(flops=1 << 12, bytes_accessed=1 << 13, transcendentals=0),
        name="inverse_rms",
    )(gathered)


def finish_kernel(scale, gathered, out_ref):
    total = jnp.sum(gathered[...], axis=0) * scale
    rows = jnp.concatenate([total[:, :CB], total[:, CB:]], 0)
    out_ref[...] = rows[:, :2 * MAX_LAG + 1]


def finish(gathered, scale):
    return pl.pallas_call(
        functools.partial(finish_kernel, scale),
        in_specs=[VMEM],
        out_specs=VMEM,
        out_shape=jax.ShapeDtypeStruct((2 * gathered.shape[1], 2 * MAX_LAG + 1), F32),
        compiler_params=pltpu.CompilerParams(vmem_limit_bytes=2 << 20),
        cost_estimate=pl.CostEstimate(flops=1 << 15, bytes_accessed=1 << 17, transcendentals=0),
        name="finish",
    )(gathered)


def exchange(block, source):
    n = lax.axis_size("chan")
    return lax.ppermute(block, "chan", [(source(i), i) for i in range(n)])


FAR = lambda i: i ^ 8
LOWER = lambda i: (i & 8) | ((i - 1) & 7)
UPPER = lambda i: (i & 8) | ((i + 1) & 7)


def local(traces, pair_bins):
    total_time = traces.shape[1] * lax.axis_size("seg")
    chan_count, seg_count = lax.axis_size("chan"), lax.axis_size("seg")
    index = lax.axis_index("chan")
    depth = index % 8
    flags = jnp.stack([index // 8, (depth == 0).astype(jnp.int32), (depth == 7).astype(jnp.int32)])
    squares = square_sums(traces)
    stream, far_payload, upper_payload, special = payloads(flags, squares, traces, pair_bins)
    with jax.named_scope("send_squares"):
        rows = [squares] + [exchange(squares, source) for source in (FAR, LOWER, UPPER)]
    rows, stream, far_payload, upper_payload = lax.optimization_barrier((rows, stream, far_payload, upper_payload))
    with jax.named_scope("send_blocks"):
        far = exchange(far_payload, FAR)
        lower = exchange(stream, LOWER)
        upper = exchange(upper_payload, UPPER)
    with jax.named_scope("energies"):
        gathered = lax.all_to_all(copies_of(rows, seg_count), "seg", 0, 0, tiled=True)
        scales = inverse_rms(gathered, total_time)
    partial_stack = fused(flags, scales, pair_bins, stream, lower, upper, far, special,
                          1.0 / math.sqrt(total_time))
    with jax.named_scope("reduce_bins"):
        slots = partial_stack.reshape(chan_count, CB // chan_count, 2 * CB)
        owned = jnp.sum(lax.all_to_all(slots, "chan", 0, 0, tiled=True), axis=0)
        copies = jnp.broadcast_to(owned[None], (seg_count,) + owned.shape)
        gathered = lax.all_to_all(copies, "seg", 0, 0, tiled=True)
        pair_total = ROUNDS * chan_count * CB * CB // NB
        return jnp.transpose(finish(gathered, 1.0 / math.sqrt(pair_total)))


def solution(mesh):
    in_specs = (P("chan", "seg"), P(None, "chan", None))
    out_specs = P(None, "chan")
    return jax.shard_map(local, mesh=mesh, in_specs=in_specs, out_specs=out_specs, check_vma=False)
```

```python
import functools
import math

import jax
import jax.numpy as jnp
from jax import lax
from jax.experimental import pallas as pl
from jax.experimental.pallas import tpu as pltpu
from jax.sharding import PartitionSpec as P

NT = (((1,), (1,)), ((), ()))
NN = (((1,), (0,)), ((), ()))
F32, BF = jnp.float32, jnp.bfloat16
W = 1152
EPSILON = 1e-06
CB = 128
VMEM = pl.BlockSpec(memory_space=pltpu.VMEM)
SMEM = pl.BlockSpec(memory_space=pltpu.SMEM)


def lag_rows(ref, start, count):
    rows = []
    for ii in range(count):
        x = jnp.broadcast_to(ref[pl.ds(start + ii, 1), :], (8, W))
        rows.append(pltpu.roll(x, 24, 1, stride=1, stride_axis=0))
    return jnp.concatenate(rows, 0).astype(BF)


def shift_rows(block, out_ref):
    for p in range(8):
        out_ref[CB * p:CB * p + CB, :] = block if p == 0 else pltpu.roll(block, 8 * p, 1)


GROUP = 8
STEP = 64


def fused_kernel(total_time, flags, squares, bins_ref, stream, lower, upper, far, special, out_ref,
                 wide, lags, shifted, c_first, c_ref, c0_ref, pair_scale, hi, lo, acc0, acc1):
    shift_rows(far[:, :W], shifted.at[0])
    wide[0] = stream[...].astype(F32)
    wide[1] = lower[...].astype(F32)
    wide[2] = upper[:, :W].astype(F32)
    iota = lax.broadcasted_iota(jnp.int32, (CB, CB), 0).astype(F32).astype(BF)
    one, zero = jnp.ones((CB, CB), BF), jnp.zeros((CB, CB), BF)
    sub = lax.broadcasted_iota(jnp.int32, (32, CB), 0) & 7
    slots = (0, flags[1], flags[2])

    def zscore(k, i, local):
        rows = c_first[pl.ds(pl.multiple_of(i * 8, 8), 8), :] if k == 0 else c_ref[k - 1, 8 * local:8 * local + 8, :]
        z = jnp.concatenate([rows[:, CB * p:CB * p + CB] for p in range(8)], 0)
        return (z * pair_scale[k, pl.ds(i, 1), :]).astype(BF)

    def low(t, i):
        return jnp.broadcast_to(lo[t, pl.ds(i, 1), :], (64, CB)).astype(BF)

    def onehot(t, i):
        return jnp.where(jnp.broadcast_to(hi[t, pl.ds(i, 1), :], (CB, CB)).astype(BF) == iota, one, zero)

    def bin_group(start, g):
        base = pl.multiple_of(start + g * GROUP, GROUP)
        rows = pl.ds(base, GROUP)
        x = [c0_ref[k, rows, :] * pair_scale[k, rows, :] for k in range(3)]
        low8 = [lo[t, rows, :] for t in range(4)]
        extra0 = jnp.concatenate([x[0], x[0] * low8[0], x[0] * low8[1], jnp.zeros_like(x[0])], 0)
        extra1 = jnp.concatenate([x[1], x[1] * low8[2], x[2], x[2] * low8[3]], 0)
        left0, left1, right0, right1 = [], [], [], []
        for ii in range(GROUP):
            i = base + ii
            e0 = jnp.where(sub == ii, extra0, 0.0).astype(BF)
            e1 = jnp.where(sub == ii, extra1, 0.0).astype(BF)
            z = [zscore(k, i, g * GROUP + ii) for k in range(3)]
            left0.append(jnp.concatenate([z[0], z[0] * low(0, i), z[0] * low(1, i), e0], 0))
            left1.append(jnp.concatenate([z[1], z[1] * low(2, i), z[2], z[2] * low(3, i), e1], 0))
            right0.append(jnp.concatenate([onehot(0, i), onehot(1, i)], 0))
            right1.append(jnp.concatenate([onehot(2, i), onehot(3, i)], 0))
        cat = lambda blocks: jnp.concatenate(blocks, 1)
        acc0[...] += lax.dot_general(cat(left0), cat(right0), NT, preferred_element_type=F32)
        acc1[...] += lax.dot_general(cat(left1), cat(right1), NT, preferred_element_type=F32)

    def prepare():
        first, last = flags[1] == 1, flags[2] == 1
        count = squares.shape[0] // 2
        low, high = jnp.sum(squares[:count], axis=0), jnp.sum(squares[count:], axis=0)
        home = jnp.where(flags[0] == 1, high, low)
        inverse_rms = lambda v: lax.rsqrt(v / total_time + EPSILON)
        near = inverse_rms(home)
        own, far_scale = near[0:1], inverse_rms(jnp.where(flags[0] == 1, low, high)[0:1])
        held = (far_scale, jnp.where(first, own, far_scale), jnp.where(last, own, far_scale))
        for t, streamed in enumerate((own, near[1:2], near[2:3])):
            column = jnp.transpose(jnp.broadcast_to(streamed, (CB, CB)))
            pair_scale[t] = column * (held[t] * (1.0 / math.sqrt(total_time)))
        sets = (far[:, W:W + CB].astype(F32), bins_ref[0].astype(F32),
                jnp.where(first, bins_ref[1].astype(F32), far[:, W + CB:].astype(F32)), upper[:, W:].astype(F32))
        for t, b in enumerate(sets):
            if t % 2 == 0:
                b = jnp.transpose(b)
            owner = jnp.floor(b * (1.0 / 16.0))
            rest = b - 16.0 * owner
            high_half = jnp.where(rest >= 8.0, 1.0, 0.0)
            hi[t] = 8.0 * owner + rest - 8.0 * high_half
            lo[t] = high_half
        acc0[...] = jnp.zeros_like(acc0)
        acc1[...] = jnp.zeros_like(acc1)
        ahead = jnp.concatenate([pltpu.roll(far[:, :W], W - 32, 1), pltpu.roll(special[...], W - 32, 1)], 0)
        for k, block in enumerate((stream[...], lower[...], upper[:, :W])):
            pair = lax.dot_general(block, ahead, NT, preferred_element_type=F32)
            c0_ref[k] = pair[:, :CB] if k == 0 else jnp.where(flags[k] == 1, pair[:, CB:], pair[:, :CB])

    lag_a, lag_b, lag_c = (lags.at[k] for k in range(3))
    half = 8 * STEP
    lag_a[...] = lag_rows(wide.at[0], 0, STEP)
    c_first[:half, :] = lax.dot_general(lag_a[...], shifted[0], NT, preferred_element_type=F32)
    shift_rows(special[...], shifted.at[1])
    lag_c[...] = lag_rows(wide.at[0], STEP, STEP)
    c_first[half:, :] = lax.dot_general(lag_c[...], shifted[0], NT, preferred_element_type=F32)
    prepare()
    lag_b[...] = lag_rows(wide.at[1], 0, STEP)

    def chunk(m, carry):
        start = m * STEP
        c_ref[0] = lax.dot_general(lag_b[...], shifted[slots[1]], NT, preferred_element_type=F32)
        lag_c[...] = lag_rows(wide.at[2], start, STEP)
        c_ref[1] = lax.dot_general(lag_c[...], shifted[slots[2]], NT, preferred_element_type=F32)
        lag_b[...] = lag_rows(wide.at[1], lax.rem(start + STEP, CB), STEP)
        for g in range(STEP // GROUP):
            bin_group(start, g)
        return carry

    lax.fori_loop(0, CB // STEP, chunk, 0)

    total = lambda v: jnp.sum(v, axis=0, keepdims=True)
    forward = [acc0[0:64, :CB] + acc1[0:64, :CB], acc0[64:128, :CB] + acc1[64:128, :CB]]
    reverse = [acc0[0:64, CB:] + acc1[128:192, CB:], acc0[128:192, CB:] + acc1[192:256, CB:]]
    forward0 = [total(acc0[192:200, :CB]) + total(acc1[256:264, :CB]), total(acc0[200:208, :CB]) + total(acc1[264:272, :CB])]
    reverse0 = [total(acc0[192:200, CB:]) + total(acc1[272:280, CB:]), total(acc0[208:216, CB:]) + total(acc1[280:288, CB:])]
    lag = lax.broadcasted_iota(jnp.int32, (CB, CB), 0)
    c = lax.broadcasted_iota(jnp.int32, (CB, CB), 1)
    r = c & 63
    m = (r >> 3) * 8 + 8 - (r & 7)
    place = jnp.where(lag == jnp.where(c < 64, m, 64 - m), 1.0, 0.0).astype(BF)
    rest = jnp.concatenate([jnp.concatenate([forward[q], reverse[q]], 0) for q in range(2)], 1)
    both = jnp.zeros((CB, 2 * CB), F32)
    for _piece in range(3):
        piece = rest.astype(BF)
        rest = rest - piece.astype(F32)
        both = both + lax.dot_general(place, piece, NN, preferred_element_type=F32)
    parts = [both[:, q * CB:q * CB + CB] + jnp.where(lag == 0, forward0[q], 0.0) + jnp.where(lag == 64, reverse0[q], 0.0)
             for q in range(2)]
    out_ref[:, :CB] = jnp.transpose(parts[0] - parts[1])
    out_ref[:, CB:] = jnp.transpose(parts[1])


def fused(flags, squares, bins, stream, lower, upper, far, special, total_time):
    return pl.pallas_call(
        functools.partial(fused_kernel, total_time),
        in_specs=[SMEM] + [VMEM] * 7,
        out_specs=VMEM,
        out_shape=jax.ShapeDtypeStruct((CB, 2 * CB), F32),
        scratch_shapes=[pltpu.VMEM((3, CB, W), F32), pltpu.VMEM((3, 8 * STEP, W), BF),
                        pltpu.VMEM((2, 1024, W), BF), pltpu.VMEM((1024, 1024), F32), pltpu.VMEM((2, 8 * STEP, 1024), F32), pltpu.VMEM((3, CB, CB), F32),
                        pltpu.VMEM((3, CB, CB), F32), pltpu.VMEM((4, CB, CB), F32), pltpu.VMEM((4, CB, CB), F32),
                        pltpu.VMEM((224, 2 * CB), F32), pltpu.VMEM((288, 2 * CB), F32)],
        compiler_params=pltpu.CompilerParams(vmem_limit_bytes=36 << 20),
        cost_estimate=pl.CostEstimate(flops=4 * 2 * 1024 * 1024 * W, bytes_accessed=6 << 20, transcendentals=0),
        name="lags_and_bins",
    )(flags, squares, bins, stream, lower, upper, far, special)


MAX_LAG = 32
NB = 256
ROUNDS = 2
HALF = 1024


def payload_kernel(flags, squares, traces, bins, stream_ref, far_ref, upper_ref, special_ref, edge, bins_v, sems):
    high, first, last = (flags[i] == 1 for i in range(3))
    mine = pl.multiple_of(jnp.where(high, HALF, 0), HALF)
    other = pl.multiple_of(HALF - mine, HALF)
    upper_start = pl.multiple_of(jnp.where(first, other, mine), HALF)
    special_start = pl.multiple_of(jnp.where(last, other, mine), HALF)
    part = lambda start: traces.at[:, pl.ds(start, HALF)]
    main = pl.ds(0, HALF)
    copies = [pltpu.make_async_copy(traces.at[:, pl.ds(HALF - CB, 2 * CB)], edge, sems.at[0]),
              pltpu.make_async_copy(bins, bins_v, sems.at[1])]
    for n, (start, ref) in enumerate(((mine, stream_ref), (other, far_ref), (upper_start, upper_ref), (special_start, special_ref))):
        copies.append(pltpu.make_async_copy(part(start), ref.at[:, main], sems.at[2 + n]))
    for copy in copies:
        copy.start()
    lane = lax.broadcasted_iota(jnp.int32, (CB, CB), 1)
    none = jnp.zeros((CB, CB), F32)
    copies[0].wait()
    halo_low = jnp.where(lane < MAX_LAG, edge[:, CB:].astype(F32), none)
    halo_high = jnp.where(lane >= CB - MAX_LAG, edge[:, :CB].astype(F32), none)
    keep_low = jnp.where(high, 0.0, 1.0)
    keep_high = 1.0 - keep_low
    stream_ref[:, HALF:] = (halo_low * keep_low).astype(BF)
    upper_ref[:, HALF:W] = (halo_low * jnp.where(first, keep_high, keep_low)).astype(BF)
    far_ref[:, HALF:W] = (halo_high * keep_low).astype(BF)
    special_ref[:, HALF:] = (halo_high * jnp.where(last, keep_low, keep_high)).astype(BF)
    copies[1].wait()
    far_ref[:, W:W + CB] = bins_v[0].astype(F32).astype(BF)
    far_ref[:, W + CB:] = bins_v[1].astype(F32).astype(BF)
    upper_ref[:, W:] = bins_v[1].astype(F32).astype(BF)
    for copy in copies[2:]:
        copy.wait()


def payloads(flags, squares, traces, bins):
    return pl.pallas_call(
        payload_kernel,
        in_specs=[SMEM, VMEM, pl.BlockSpec(memory_space=pl.ANY), pl.BlockSpec(memory_space=pl.ANY)],
        out_specs=[VMEM] * 4,
        out_shape=[jax.ShapeDtypeStruct((CB, width), BF) for width in (W, W + 2 * CB, W + CB, W)],
        scratch_shapes=[pltpu.VMEM((CB, 2 * CB), BF), pltpu.VMEM((2, CB, CB), jnp.int32), pltpu.SemaphoreType.DMA((6,))],
        compiler_params=pltpu.CompilerParams(vmem_limit_bytes=8 << 20),
        cost_estimate=pl.CostEstimate(flops=1 << 18, bytes_accessed=2 << 20, transcendentals=0),
        name="payloads",
    )(flags, squares, traces, bins)


def square_kernel(traces, out_ref):
    total = jnp.zeros((CB, CB), F32)
    for t in range(2 * HALF // CB):
        x = traces[:, CB * t:CB * t + CB].astype(F32)
        total = total + x * x
    out_ref[...] = jnp.sum(jnp.transpose(total), axis=0, keepdims=True)


def square_sums(traces):
    return pl.pallas_call(
        square_kernel,
        in_specs=[VMEM],
        out_specs=VMEM,
        out_shape=jax.ShapeDtypeStruct((1, CB), F32),
        compiler_params=pltpu.CompilerParams(vmem_limit_bytes=4 << 20),
        cost_estimate=pl.CostEstimate(flops=1 << 18, bytes_accessed=1 << 19, transcendentals=0),
        name="square_sums",
    )(traces)


def copies_kernel(*refs):
    rows = jnp.concatenate([ref[...] for ref in refs[:-1]], 0)
    refs[-1][...] = jnp.broadcast_to(rows[None], refs[-1].shape)


def copies_of(rows, count):
    return pl.pallas_call(
        copies_kernel,
        in_specs=[VMEM] * len(rows),
        out_specs=VMEM,
        out_shape=jax.ShapeDtypeStruct((count, len(rows), CB), F32),
        compiler_params=pltpu.CompilerParams(vmem_limit_bytes=2 << 20),
        cost_estimate=pl.CostEstimate(flops=1 << 12, bytes_accessed=1 << 15, transcendentals=0),
        name="square_copies",
    )(*rows)


def finish_kernel(scale, gathered, out_ref):
    total = jnp.sum(gathered[...], axis=0) * scale
    rows = jnp.concatenate([total[:, :CB], total[:, CB:]], 0)
    out_ref[...] = rows[:, :2 * MAX_LAG + 1]


def finish(gathered, scale):
    return pl.pallas_call(
        functools.partial(finish_kernel, scale),
        in_specs=[VMEM],
        out_specs=VMEM,
        out_shape=jax.ShapeDtypeStruct((2 * gathered.shape[1], 2 * MAX_LAG + 1), F32),
        compiler_params=pltpu.CompilerParams(vmem_limit_bytes=2 << 20),
        cost_estimate=pl.CostEstimate(flops=1 << 15, bytes_accessed=1 << 17, transcendentals=0),
        name="finish",
    )(gathered)


def exchange(block, source):
    n = lax.axis_size("chan")
    return lax.ppermute(block, "chan", [(source(i), i) for i in range(n)])


FAR = lambda i: i ^ 8
LOWER = lambda i: (i & 8) | ((i - 1) & 7)
UPPER = lambda i: (i & 8) | ((i + 1) & 7)


def local(traces, pair_bins):
    total_time = traces.shape[1] * lax.axis_size("seg")
    chan_count, seg_count = lax.axis_size("chan"), lax.axis_size("seg")
    index = lax.axis_index("chan")
    depth = index % 8
    flags = jnp.stack([index // 8, (depth == 0).astype(jnp.int32), (depth == 7).astype(jnp.int32)])
    squares = square_sums(traces)
    stream, far_payload, upper_payload, special = payloads(flags, squares, traces, pair_bins)
    with jax.named_scope("send_squares"):
        rows = [squares] + [exchange(squares, source) for source in (LOWER, UPPER)]
    rows, stream, far_payload, upper_payload = lax.optimization_barrier((rows, stream, far_payload, upper_payload))
    with jax.named_scope("send_blocks"):
        far = exchange(far_payload, FAR)
        lower = exchange(stream, LOWER)
        upper = exchange(upper_payload, UPPER)
    with jax.named_scope("energies"):
        block = lambda c: [c * seg_count + n for n in range(seg_count)]
        groups = [block(c) + block(FAR(c)) for c in range(chan_count // 2)]
        gathered = lax.all_to_all(copies_of(rows, 2 * seg_count), ("chan", "seg"), 0, 0, tiled=True, axis_index_groups=groups)
    partial_stack = fused(flags, gathered, pair_bins, stream, lower, upper, far, special, total_time)
    with jax.named_scope("reduce_bins"):
        slots = partial_stack.reshape(chan_count, CB // chan_count, 2 * CB)
        owned = jnp.sum(lax.all_to_all(slots, "chan", 0, 0, tiled=True), axis=0)
        copies = jnp.broadcast_to(owned[None], (seg_count,) + owned.shape)
        gathered = lax.all_to_all(copies, "seg", 0, 0, tiled=True)
        pair_total = ROUNDS * chan_count * CB * CB // NB
        return jnp.transpose(finish(gathered, 1.0 / math.sqrt(pair_total)))


def solution(mesh):
    in_specs = (P("chan", "seg"), P(None, "chan", None))
    out_specs = P(None, "chan")
    return jax.shard_map(local, mesh=mesh, in_specs=in_specs, out_specs=out_specs, check_vma=False)
```

```python
import functools
import math

import jax
import jax.numpy as jnp
from jax import lax
from jax.experimental import pallas as pl
from jax.experimental.pallas import tpu as pltpu
from jax.sharding import PartitionSpec as P

NT = (((1,), (1,)), ((), ()))
NN = (((1,), (0,)), ((), ()))
F32, BF = jnp.float32, jnp.bfloat16
W = 1152
EPSILON = 1e-06
CB = 128
VMEM = pl.BlockSpec(memory_space=pltpu.VMEM)
SMEM = pl.BlockSpec(memory_space=pltpu.SMEM)


def lag_rows(ref, start, count):
    rows = []
    for ii in range(count):
        x = jnp.broadcast_to(ref[pl.ds(start + ii, 1), :], (8, W))
        rows.append(pltpu.roll(x, 24, 1, stride=1, stride_axis=0))
    return jnp.concatenate(rows, 0).astype(BF)


def shift_rows(block, out_ref):
    for p in range(8):
        out_ref[CB * p:CB * p + CB, :] = block if p == 0 else pltpu.roll(block, 8 * p, 1)


GROUP = 8
STEP = 64


def fused_kernel(total_time, flags, squares, bins_ref, stream, lower, upper, far, special, out_ref,
                 wide, lags, shifted, c_first, c_ref, c0_ref, pair_scale, hi, lo, acc0, acc1):
    shift_rows(far[:, :W], shifted.at[0])
    wide[0] = stream[...].astype(F32)
    wide[1] = lower[...].astype(F32)
    wide[2] = upper[:, :W].astype(F32)
    iota = lax.broadcasted_iota(jnp.int32, (CB, CB), 0).astype(F32).astype(BF)
    one, zero = jnp.ones((CB, CB), BF), jnp.zeros((CB, CB), BF)
    sub = lax.broadcasted_iota(jnp.int32, (32, CB), 0) & 7
    slots = (0, flags[1], flags[2])

    def zscore(k, i, local):
        rows = c_first[pl.ds(pl.multiple_of(i * 8, 8), 8), :] if k == 0 else c_ref[k - 1, 8 * local:8 * local + 8, :]
        z = jnp.concatenate([rows[:, CB * p:CB * p + CB] for p in range(8)], 0)
        return (z * pair_scale[k, pl.ds(i, 1), :]).astype(BF)

    def low(t, i):
        return jnp.broadcast_to(lo[t, pl.ds(i, 1), :], (64, CB)).astype(BF)

    def onehot(t, i):
        return jnp.where(jnp.broadcast_to(hi[t, pl.ds(i, 1), :], (CB, CB)).astype(BF) == iota, one, zero)

    def bin_group(start, g):
        base = pl.multiple_of(start + g * GROUP, GROUP)
        rows = pl.ds(base, GROUP)
        x = [c0_ref[k, rows, :] * pair_scale[k, rows, :] for k in range(3)]
        low8 = [lo[t, rows, :] for t in range(4)]
        extra0 = jnp.concatenate([x[0], x[0] * low8[0], x[0] * low8[1], jnp.zeros_like(x[0])], 0)
        extra1 = jnp.concatenate([x[1], x[1] * low8[2], x[2], x[2] * low8[3]], 0)
        left0, left1, right0, right1 = [], [], [], []
        for ii in range(GROUP):
            i = base + ii
            e0 = jnp.where(sub == ii, extra0, 0.0).astype(BF)
            e1 = jnp.where(sub == ii, extra1, 0.0).astype(BF)
            z = [zscore(k, i, g * GROUP + ii) for k in range(3)]
            left0.append(jnp.concatenate([z[0], z[0] * low(0, i), z[0] * low(1, i), e0], 0))
            left1.append(jnp.concatenate([z[1], z[1] * low(2, i), z[2], z[2] * low(3, i), e1], 0))
            right0.append(jnp.concatenate([onehot(0, i), onehot(1, i)], 0))
            right1.append(jnp.concatenate([onehot(2, i), onehot(3, i)], 0))
        cat = lambda blocks: jnp.concatenate(blocks, 1)
        acc0[...] += lax.dot_general(cat(left0), cat(right0), NT, preferred_element_type=F32)
        acc1[...] += lax.dot_general(cat(left1), cat(right1), NT, preferred_element_type=F32)

    def prepare():
        first, last = flags[1] == 1, flags[2] == 1
        count = squares.shape[0] // 2
        low, high = jnp.sum(squares[:count], axis=0), jnp.sum(squares[count:], axis=0)
        home = jnp.where(flags[0] == 1, high, low)
        inverse_rms = lambda v: lax.rsqrt(v / total_time + EPSILON)
        near = inverse_rms(home)
        own, far_scale = near[:, :CB], inverse_rms(jnp.where(flags[0] == 1, low, high)[:, :CB])
        held = (far_scale, jnp.where(first, own, far_scale), jnp.where(last, own, far_scale))
        for t, streamed in enumerate((own, near[:, CB:2 * CB], near[:, 2 * CB:])):
            column = jnp.transpose(jnp.broadcast_to(streamed, (CB, CB)))
            pair_scale[t] = column * (held[t] * (1.0 / math.sqrt(total_time)))
        sets = (far[:, W:W + CB].astype(F32), bins_ref[0].astype(F32),
                jnp.where(first, bins_ref[1].astype(F32), far[:, W + CB:].astype(F32)), upper[:, W:].astype(F32))
        for t, b in enumerate(sets):
            if t % 2 == 0:
                b = jnp.transpose(b)
            owner = jnp.floor(b * (1.0 / 16.0))
            rest = b - 16.0 * owner
            high_half = jnp.where(rest >= 8.0, 1.0, 0.0)
            hi[t] = 8.0 * owner + rest - 8.0 * high_half
            lo[t] = high_half
        acc0[...] = jnp.zeros_like(acc0)
        acc1[...] = jnp.zeros_like(acc1)
        ahead = jnp.concatenate([pltpu.roll(far[:, :W], W - 32, 1), pltpu.roll(special[...], W - 32, 1)], 0)
        for k, block in enumerate((stream[...], lower[...], upper[:, :W])):
            pair = lax.dot_general(block, ahead, NT, preferred_element_type=F32)
            c0_ref[k] = pair[:, :CB] if k == 0 else jnp.where(flags[k] == 1, pair[:, CB:], pair[:, :CB])

    lag_a, lag_b, lag_c = (lags.at[k] for k in range(3))
    half = 8 * STEP
    lag_a[...] = lag_rows(wide.at[0], 0, STEP)
    c_first[:half, :] = lax.dot_general(lag_a[...], shifted[0], NT, preferred_element_type=F32)
    shift_rows(special[...], shifted.at[1])
    lag_c[...] = lag_rows(wide.at[0], STEP, STEP)
    c_first[half:, :] = lax.dot_general(lag_c[...], shifted[0], NT, preferred_element_type=F32)
    prepare()
    lag_b[...] = lag_rows(wide.at[1], 0, STEP)

    def chunk(m, carry):
        start = m * STEP
        c_ref[0] = lax.dot_general(lag_b[...], shifted[slots[1]], NT, preferred_element_type=F32)
        lag_c[...] = lag_rows(wide.at[2], start, STEP)
        c_ref[1] = lax.dot_general(lag_c[...], shifted[slots[2]], NT, preferred_element_type=F32)
        lag_b[...] = lag_rows(wide.at[1], lax.rem(start + STEP, CB), STEP)
        for g in range(STEP // GROUP):
            bin_group(start, g)
        return carry

    lax.fori_loop(0, CB // STEP, chunk, 0)

    total = lambda v: jnp.sum(v, axis=0, keepdims=True)
    forward = [acc0[0:64, :CB] + acc1[0:64, :CB], acc0[64:128, :CB] + acc1[64:128, :CB]]
    reverse = [acc0[0:64, CB:] + acc1[128:192, CB:], acc0[128:192, CB:] + acc1[192:256, CB:]]
    forward0 = [total(acc0[192:200, :CB]) + total(acc1[256:264, :CB]), total(acc0[200:208, :CB]) + total(acc1[264:272, :CB])]
    reverse0 = [total(acc0[192:200, CB:]) + total(acc1[272:280, CB:]), total(acc0[208:216, CB:]) + total(acc1[280:288, CB:])]
    lag = lax.broadcasted_iota(jnp.int32, (CB, CB), 0)
    c = lax.broadcasted_iota(jnp.int32, (CB, CB), 1)
    r = c & 63
    m = (r >> 3) * 8 + 8 - (r & 7)
    place = jnp.where(lag == jnp.where(c < 64, m, 64 - m), 1.0, 0.0).astype(BF)
    rest = jnp.concatenate([jnp.concatenate([forward[q], reverse[q]], 0) for q in range(2)], 1)
    both = jnp.zeros((CB, 2 * CB), F32)
    for _piece in range(3):
        piece = rest.astype(BF)
        rest = rest - piece.astype(F32)
        both = both + lax.dot_general(place, piece, NN, preferred_element_type=F32)
    parts = [both[:, q * CB:q * CB + CB] + jnp.where(lag == 0, forward0[q], 0.0) + jnp.where(lag == 64, reverse0[q], 0.0)
             for q in range(2)]
    out_ref[:, :CB] = jnp.transpose(parts[0] - parts[1])
    out_ref[:, CB:] = jnp.transpose(parts[1])


def fused(flags, squares, bins, stream, lower, upper, far, special, total_time):
    return pl.pallas_call(
        functools.partial(fused_kernel, total_time),
        in_specs=[SMEM] + [VMEM] * 7,
        out_specs=VMEM,
        out_shape=jax.ShapeDtypeStruct((CB, 2 * CB), F32),
        scratch_shapes=[pltpu.VMEM((3, CB, W), F32), pltpu.VMEM((3, 8 * STEP, W), BF),
                        pltpu.VMEM((2, 1024, W), BF), pltpu.VMEM((1024, 1024), F32), pltpu.VMEM((2, 8 * STEP, 1024), F32), pltpu.VMEM((3, CB, CB), F32),
                        pltpu.VMEM((3, CB, CB), F32), pltpu.VMEM((4, CB, CB), F32), pltpu.VMEM((4, CB, CB), F32),
                        pltpu.VMEM((224, 2 * CB), F32), pltpu.VMEM((288, 2 * CB), F32)],
        compiler_params=pltpu.CompilerParams(vmem_limit_bytes=36 << 20),
        cost_estimate=pl.CostEstimate(flops=4 * 2 * 1024 * 1024 * W, bytes_accessed=6 << 20, transcendentals=0),
        name="lags_and_bins",
    )(flags, squares, bins, stream, lower, upper, far, special)


MAX_LAG = 32
NB = 256
ROUNDS = 2
HALF = 1024


def payload_kernel(flags, squares, traces, bins, stream_ref, far_ref, upper_ref, special_ref, edge, bins_v, sems):
    high, first, last = (flags[i] == 1 for i in range(3))
    mine = pl.multiple_of(jnp.where(high, HALF, 0), HALF)
    other = pl.multiple_of(HALF - mine, HALF)
    upper_start = pl.multiple_of(jnp.where(first, other, mine), HALF)
    special_start = pl.multiple_of(jnp.where(last, other, mine), HALF)
    part = lambda start: traces.at[:, pl.ds(start, HALF)]
    main = pl.ds(0, HALF)
    copies = [pltpu.make_async_copy(traces.at[:, pl.ds(HALF - CB, 2 * CB)], edge, sems.at[0]),
              pltpu.make_async_copy(bins, bins_v, sems.at[1])]
    for n, (start, ref) in enumerate(((mine, stream_ref), (other, far_ref), (upper_start, upper_ref), (special_start, special_ref))):
        copies.append(pltpu.make_async_copy(part(start), ref.at[:, main], sems.at[2 + n]))
    for copy in copies:
        copy.start()
    lane = lax.broadcasted_iota(jnp.int32, (CB, CB), 1)
    none = jnp.zeros((CB, CB), F32)
    copies[0].wait()
    halo_low = jnp.where(lane < MAX_LAG, edge[:, CB:].astype(F32), none)
    halo_high = jnp.where(lane >= CB - MAX_LAG, edge[:, :CB].astype(F32), none)
    keep_low = jnp.where(high, 0.0, 1.0)
    keep_high = 1.0 - keep_low
    stream_ref[:, HALF:] = (halo_low * keep_low).astype(BF)
    upper_ref[:, HALF:W] = (halo_low * jnp.where(first, keep_high, keep_low)).astype(BF)
    far_ref[:, HALF:W] = (halo_high * keep_low).astype(BF)
    special_ref[:, HALF:] = (halo_high * jnp.where(last, keep_low, keep_high)).astype(BF)
    copies[1].wait()
    far_ref[:, W:W + CB] = bins_v[0].astype(F32).astype(BF)
    far_ref[:, W + CB:] = bins_v[1].astype(F32).astype(BF)
    upper_ref[:, W:] = bins_v[1].astype(F32).astype(BF)
    for copy in copies[2:]:
        copy.wait()


def payloads(flags, squares, traces, bins):
    return pl.pallas_call(
        payload_kernel,
        in_specs=[SMEM, VMEM, pl.BlockSpec(memory_space=pl.ANY), pl.BlockSpec(memory_space=pl.ANY)],
        out_specs=[VMEM] * 4,
        out_shape=[jax.ShapeDtypeStruct((CB, width), BF) for width in (W, W + 2 * CB, W + CB, W)],
        scratch_shapes=[pltpu.VMEM((CB, 2 * CB), BF), pltpu.VMEM((2, CB, CB), jnp.int32), pltpu.SemaphoreType.DMA((6,))],
        compiler_params=pltpu.CompilerParams(vmem_limit_bytes=8 << 20),
        cost_estimate=pl.CostEstimate(flops=1 << 18, bytes_accessed=2 << 20, transcendentals=0),
        name="payloads",
    )(flags, squares, traces, bins)


def square_kernel(traces, out_ref):
    total = jnp.zeros((CB, CB), F32)
    for t in range(2 * HALF // CB):
        x = traces[:, CB * t:CB * t + CB].astype(F32)
        total = total + x * x
    out_ref[...] = jnp.sum(jnp.transpose(total), axis=0, keepdims=True)


def square_sums(traces):
    return pl.pallas_call(
        square_kernel,
        in_specs=[VMEM],
        out_specs=VMEM,
        out_shape=jax.ShapeDtypeStruct((1, CB), F32),
        compiler_params=pltpu.CompilerParams(vmem_limit_bytes=4 << 20),
        cost_estimate=pl.CostEstimate(flops=1 << 18, bytes_accessed=1 << 19, transcendentals=0),
        name="square_sums",
    )(traces)


def copies_kernel(*refs):
    rows = jnp.concatenate([ref[...] for ref in refs[:-1]], 1)
    refs[-1][...] = jnp.broadcast_to(rows[None], refs[-1].shape)


def copies_of(rows, count):
    return pl.pallas_call(
        copies_kernel,
        in_specs=[VMEM] * len(rows),
        out_specs=VMEM,
        out_shape=jax.ShapeDtypeStruct((count, 1, len(rows) * CB), F32),
        compiler_params=pltpu.CompilerParams(vmem_limit_bytes=2 << 20),
        cost_estimate=pl.CostEstimate(flops=1 << 12, bytes_accessed=1 << 15, transcendentals=0),
        name="square_copies",
    )(*rows)


def finish_kernel(scale, gathered, out_ref):
    total = jnp.sum(gathered[...], axis=0) * scale
    rows = jnp.concatenate([total[:, :CB], total[:, CB:]], 0)
    out_ref[...] = rows[:, :2 * MAX_LAG + 1]


def finish(gathered, scale):
    return pl.pallas_call(
        functools.partial(finish_kernel, scale),
        in_specs=[VMEM],
        out_specs=VMEM,
        out_shape=jax.ShapeDtypeStruct((2 * gathered.shape[1], 2 * MAX_LAG + 1), F32),
        compiler_params=pltpu.CompilerParams(vmem_limit_bytes=2 << 20),
        cost_estimate=pl.CostEstimate(flops=1 << 15, bytes_accessed=1 << 17, transcendentals=0),
        name="finish",
    )(gathered)


def exchange(block, source):
    n = lax.axis_size("chan")
    return lax.ppermute(block, "chan", [(source(i), i) for i in range(n)])


FAR = lambda i: i ^ 8
LOWER = lambda i: (i & 8) | ((i - 1) & 7)
UPPER = lambda i: (i & 8) | ((i + 1) & 7)


def local(traces, pair_bins):
    total_time = traces.shape[1] * lax.axis_size("seg")
    chan_count, seg_count = lax.axis_size("chan"), lax.axis_size("seg")
    index = lax.axis_index("chan")
    depth = index % 8
    flags = jnp.stack([index // 8, (depth == 0).astype(jnp.int32), (depth == 7).astype(jnp.int32)])
    squares = square_sums(traces)
    stream, far_payload, upper_payload, special = payloads(flags, squares, traces, pair_bins)
    with jax.named_scope("send_squares"):
        rows = [squares] + [exchange(squares, source) for source in (LOWER, UPPER)]
    rows, stream, far_payload, upper_payload = lax.optimization_barrier((rows, stream, far_payload, upper_payload))
    with jax.named_scope("send_blocks"):
        far = exchange(far_payload, FAR)
        lower = exchange(stream, LOWER)
        upper = exchange(upper_payload, UPPER)
    with jax.named_scope("energies"):
        block = lambda c: [c * seg_count + n for n in range(seg_count)]
        groups = [block(c) + block(FAR(c)) for c in range(chan_count // 2)]
        gathered = lax.all_to_all(copies_of(rows, 2 * seg_count), ("chan", "seg"), 0, 0, tiled=True, axis_index_groups=groups)
    partial_stack = fused(flags, gathered, pair_bins, stream, lower, upper, far, special, total_time)
    with jax.named_scope("reduce_bins"):
        slots = partial_stack.reshape(chan_count, CB // chan_count, 2 * CB)
        owned = jnp.sum(lax.all_to_all(slots, "chan", 0, 0, tiled=True), axis=0)
        copies = jnp.broadcast_to(owned[None], (seg_count,) + owned.shape)
        gathered = lax.all_to_all(copies, "seg", 0, 0, tiled=True)
        pair_total = ROUNDS * chan_count * CB * CB // NB
        return jnp.transpose(finish(gathered, 1.0 / math.sqrt(pair_total)))


def solution(mesh):
    in_specs = (P("chan", "seg"), P(None, "chan", None))
    out_specs = P(None, "chan")
    return jax.shard_map(local, mesh=mesh, in_specs=in_specs, out_specs=out_specs, check_vma=False)
```
